256 devices in a mesh: tile: 32 (over y, x, core), rep: 8 (over z).
Axes of the slice: x: 4, y: 4, z: 8, core: 2. Of those that a mesh axis runs over, the one named last changes fastest.
Arguments:
- tile_data: bfloat16 [8, 128, 16, 16, 192], P('rep', 'tile'), may hold values from -6 to 6
- cotangent: bfloat16 [8, 128, 16, 16, 192], P('rep', 'tile'), may hold values from -6 to 6
- tile_place: int32 [8, 32, 4], P('rep', 'tile'), may hold values from 0 to 3, each once within a row
- tile_count: int32 [8, 32], P('rep', 'tile'), may hold values from 1 to 4, as said below
- kernel: float32 [7, 7, 192], replicated, may hold values from -0.875 to 0.875
- norm_gain: float32 [192], replicated, may hold values from 0.5 to 1.5
- expand_weight: bfloat16 [192, 768], P('rep'), may hold values from -0.4375 to 0.4375
- hidden_bias: float32 [768], replicated, may hold values from -3 to 3
- reduce_weight: bfloat16 [768, 192], P('rep'), may hold values from -0.21875 to 0.21875
Outputs:
- result_tiles: float32 [8, 128, 16, 16, 192], P('rep', 'tile')
- grad_tiles: float32 [8, 128, 16, 16, 192], P('rep', 'tile')
- grad_expand: float32 [192, 768], P('rep')
- grad_reduce: float32 [768, 192], P('rep')
- grad_kernel: float32 [7, 7, 192], replicated
The draws below stay inside these ranges and needn't reach their ends.
Inputs may be any that keep to these rules, and one draw needn't show every extreme that they name: In every slide device d keeps its tiles in slots 0 to tile_count[d] - 1, and some device holds 4 tiles. `tile_place`: each row lists every block position once.
All inputs are finite; a program needn't handle non-finite values.
Results may differ from the reference program's by a relative error of at most 0.007.
Values may be sent and summed in bfloat16 or wider, within the bound.
No kernel may reach another device: no remote copies, remote signals or barrier semaphores. Data moves between devices by JAX's collectives and lax.ppermute only.
A program may use at most 64 MiB of HBM per device.

```python
import math
import jax
import jax.numpy as jnp
from jax import lax

C = 192
FF = 768
S = 16
CAP = 4
KS = 7
REG_COLS = 4
SLIDES = 8
TSLOTS = 128
N_TILE = 32


def draw_tile_count(key, part):
    key = jax.random.fold_in(key, 11)
    first_draw = jax.random.randint(jax.random.fold_in(key, 1), (SLIDES, N_TILE), 1, CAP + 1)
    second_draw = jax.random.randint(jax.random.fold_in(key, 2), (SLIDES, N_TILE), 1, CAP + 1)
    tile_counts = jnp.minimum(first_draw, second_draw)
    full_device = jax.random.randint(jax.random.fold_in(key, 3), (SLIDES,), 0, N_TILE)
    tile_counts = tile_counts.at[jnp.arange(SLIDES), full_device].set(CAP)
    return tile_counts.astype(jnp.int32)


def levels(rng, dims, split, smallest, largest):
    factor_of, own = 1.0, jax.random.fold_in(rng, 6)
    for position, parts in split:
        heights = jnp.exp(jax.random.uniform(jax.random.fold_in(own, position), (parts,), jnp.float32, smallest / len(split), largest / len(split)))
        factor_of = factor_of * jnp.repeat(heights, dims[position] // parts).reshape([-1 if axis == position else 1 for axis in range(len(dims))])
    return factor_of


def normal_values(key, shape, deviation, reach, pieces=(), dtype=jnp.bfloat16):
    gain = levels(key, shape, pieces, -0.22, 0.18) if pieces else 1.0
    values = jax.random.normal(key, shape, jnp.float32) * deviation * gain
    return jnp.minimum(jnp.maximum(values, -reach), reach).astype(dtype)


def setup_inputs(seed: int = 0) -> dict:
    key_of = jax.random.split(jax.random.key(seed), 10)
    return {
        "tile_data": normal_values(key_of[0], (SLIDES, TSLOTS, S, S, C), 1.0, 6.0, ((0, 8), (1, 32))),
        "cotangent": normal_values(key_of[1], (SLIDES, TSLOTS, S, S, C), 1.0, 6.0, ((0, 8), (1, 32))),
        "tile_place": jax.vmap(lambda own: jax.random.permutation(own, CAP))(jax.random.split(key_of[2], SLIDES * N_TILE)).reshape((SLIDES, N_TILE, CAP)).astype(jnp.int32),
        "tile_count": draw_tile_count(jax.random.fold_in(key_of[9], 71), 0),
        "kernel": normal_values(key_of[4], (KS, KS, C), (KS * KS) ** -0.5, 0.875, (), jnp.float32),
        "norm_gain": jnp.clip(1.0 + 0.1 * jax.random.normal(key_of[5], (C,), jnp.float32), 0.5, 1.5),
        "expand_weight": normal_values(key_of[6], (C, FF), C ** -0.5, 0.4375, ((0, 8),)),
        "hidden_bias": normal_values(key_of[7], (FF,), 0.5, 3.0, (), jnp.float32),
        "reduce_weight": normal_values(key_of[8], (FF, C), FF ** -0.5, 0.21875, ((0, 8),)),
    }


conv_dims = ('NHWC', 'HWIO', 'NHWC')
inv_root_two = 0.7071067811865476
inv_root_two_pi = 0.3989422804014327

def depthwise(padded, kernel):
    output = lax.conv_general_dilated(padded[None], kernel[:, :, None, :], (1, 1), 'VALID', dimension_numbers=conv_dims, feature_group_count=padded.shape[-1], precision=lax.Precision.HIGHEST)
    return output[0]

def row_contract(left, right):
    return lax.dot_general(left, right, (((0,), (0,)), ((), ())), preferred_element_type=jnp.float32)

def right_contract(left, right):
    return lax.dot_general(left, right, (((1,), (1,)), ((), ())), preferred_element_type=jnp.float32)

def forward_backward(padded, live_mask, cotan_canvas, kernel, norm_gain, expand_weight, hidden_bias, reduce_weight):
    row_count, col_count, channels = cotan_canvas.shape
    cell_count = row_count * col_count
    canvas = padded[3:-3, 3:-3, :].reshape(cell_count, channels)
    filtered = depthwise(padded.astype(jnp.float32), kernel).reshape(cell_count, channels)
    centre = lax.optimization_barrier(jnp.mean(filtered, axis=1, keepdims=True))
    spread = filtered - centre
    inverse_spread = lax.rsqrt(lax.optimization_barrier(jnp.mean(spread * spread, axis=1, keepdims=True)) + 1e-06)
    normed = spread * inverse_spread
    scaled = (normed * norm_gain).astype(jnp.bfloat16)
    hidden_in = jnp.dot(scaled, expand_weight, preferred_element_type=jnp.float32) + hidden_bias
    normal_cdf = 0.5 * (1.0 + lax.erf(hidden_in * inv_root_two))
    active = (hidden_in * normal_cdf).astype(jnp.bfloat16)
    mixed = jnp.dot(active, reduce_weight, preferred_element_type=jnp.float32)
    mask_rows = live_mask.reshape(cell_count, 1)
    result = (canvas.astype(jnp.float32) + mixed) * mask_rows.astype(jnp.float32)
    upstream = cotan_canvas.reshape(cell_count, channels) * mask_rows
    grad_reduce = row_contract(active, upstream)
    grad_active = right_contract(upstream, reduce_weight)
    gelu_slope = normal_cdf + hidden_in * jnp.exp(-0.5 * hidden_in * hidden_in) * inv_root_two_pi
    grad_hidden = (grad_active * gelu_slope).astype(jnp.bfloat16)
    grad_expand = row_contract(scaled, grad_hidden)
    grad_scaled = right_contract(grad_hidden, expand_weight) * norm_gain
    grad_field = inverse_spread * (grad_scaled - lax.optimization_barrier(jnp.mean(grad_scaled, axis=1, keepdims=True)) - normed * lax.optimization_barrier(jnp.mean(grad_scaled * normed, axis=1, keepdims=True)))
    grad_field = grad_field.astype(jnp.bfloat16).reshape(row_count, col_count, channels)
    return (result.reshape(row_count, col_count, channels), upstream.reshape(row_count, col_count, channels), grad_field, grad_expand, grad_reduce)

def slide_image(tile_block, onehot):
    block_rows = N_TILE // REG_COLS
    placed = jnp.einsum('djp,djxyc->dpxyc', onehot, tile_block.reshape(N_TILE, CAP, S, S, -1).astype(jnp.float32))
    placed = placed.reshape(block_rows, REG_COLS, 2, 2, S, S, -1).transpose(0, 2, 4, 1, 3, 5, 6)
    return placed.reshape(block_rows * 2 * S, REG_COLS * 2 * S, -1).astype(jnp.bfloat16)

def slide_tiles(canvas, onehot):
    block_rows = N_TILE // REG_COLS
    blocks = canvas.astype(jnp.float32).reshape(block_rows, 2, S, REG_COLS, 2, S, -1).transpose(0, 3, 1, 4, 2, 5, 6)
    blocks = blocks.reshape(N_TILE, CAP, S, S, -1)
    placed = jnp.einsum('djp,dpxyc->djxyc', onehot, blocks)
    return placed.reshape(TSLOTS, S, S, -1)

def reference(tile_data, cotangent, tile_place, tile_count, kernel, norm_gain, expand_weight, hidden_bias, reduce_weight):

    def one_slide(inputs):
        slide_data, slide_cotan, slide_place, slide_count = inputs
        positions = jnp.arange(CAP).astype(jnp.int32)
        live_slots = (positions[None, :] < slide_count[:, None]).astype(jnp.float32)
        onehot = (slide_place[:, :, None] == positions[None, None, :]).astype(jnp.float32) * live_slots[:, :, None]
        canvas = slide_image(slide_data, onehot)
        cotan_canvas = slide_image(slide_cotan, onehot)
        live_mask = slide_image(jnp.ones((TSLOTS, S, S, 1), jnp.bfloat16), onehot)
        padded = jnp.pad(canvas, ((3, 3), (3, 3), (0, 0)))
        result, upstream, grad_field, grad_expand, grad_reduce = forward_backward(padded, live_mask, cotan_canvas, kernel, norm_gain, expand_weight, hidden_bias, reduce_weight)
        grad_padded = jnp.pad(grad_field, ((3, 3), (3, 3), (0, 0)))
        grad_canvas = upstream.astype(jnp.float32) + depthwise(grad_padded.astype(jnp.float32), kernel[::-1, ::-1])
        grad_canvas = grad_canvas * live_mask.astype(jnp.float32)
        grad_kern = depthwise(padded.astype(jnp.float32), grad_field.astype(jnp.float32))
        return (slide_tiles(result, onehot), slide_tiles(grad_canvas, onehot), grad_expand, grad_reduce, grad_kern)
    outputs = lax.map(one_slide, (tile_data, cotangent, tile_place, tile_count))
    factor = 1.0 / math.sqrt(SLIDES * TSLOTS * S * S)
    return (outputs[0], outputs[1], lax.optimization_barrier(jnp.sum(outputs[2], axis=0)) * factor, lax.optimization_barrier(jnp.sum(outputs[3], axis=0)) * factor, lax.optimization_barrier(jnp.sum(outputs[4], axis=0)) * factor)
```

```python
import math

import jax
import jax.numpy as jnp
from jax import lax
from jax.sharding import Mesh, PartitionSpec as P

conv_dims = ("NHWC", "HWIO", "NHWC")
inv_root_two = 0.7071067811865476
inv_root_two_pi = 0.3989422804014327
bf16 = jnp.bfloat16
f32 = jnp.float32
TILE = ("y", "x", "core")
SIZES = {"y": 4, "x": 4, "core": 2, "rep": 8}


def swap(value, axis, bit):
    return lax.ppermute(value, axis, [(i, i ^ bit) for i in range(SIZES[axis])])


def bit_of(axis, bit):
    return (lax.axis_index(axis) // bit) % 2


def depthwise(padded, kernel):
    output = lax.conv_general_dilated(
        padded[None],
        kernel[:, :, None, :],
        (1, 1),
        "VALID",
        dimension_numbers=conv_dims,
        feature_group_count=padded.shape[-1],
        precision=lax.Precision.HIGHEST,
    )
    return output[0]


def row_contract(left, right):
    return lax.dot_general(left, right, (((0,), (0,)), ((), ())), preferred_element_type=f32)


def right_contract(left, right):
    return lax.dot_general(left, right, (((1,), (1,)), ((), ())), preferred_element_type=f32)


def forward_backward(
    padded, live_mask, cotan_canvas, kernel, norm_gain, expand_weight, hidden_bias, reduce_weight
):
    row_count, col_count, channels = cotan_canvas.shape
    cell_count = row_count * col_count
    canvas = padded[3:-3, 3:-3, :].reshape(cell_count, channels)
    filtered = depthwise(padded.astype(f32), kernel).reshape(cell_count, channels)
    centre = jnp.mean(filtered, axis=1, keepdims=True)
    spread = filtered - centre
    inverse_spread = lax.rsqrt(jnp.mean(spread * spread, axis=1, keepdims=True) + 1e-06)
    normed = spread * inverse_spread
    scaled = (normed * norm_gain).astype(bf16)
    hidden_in = jnp.dot(scaled, expand_weight, preferred_element_type=f32) + hidden_bias
    normal_cdf = 0.5 * (1.0 + lax.erf(hidden_in * inv_root_two))
    active = (hidden_in * normal_cdf).astype(bf16)
    mixed = jnp.dot(active, reduce_weight, preferred_element_type=f32)
    mask_rows = live_mask.reshape(cell_count, 1)
    result = (canvas.astype(f32) + mixed) * mask_rows.astype(f32)
    upstream = cotan_canvas.reshape(cell_count, channels) * mask_rows
    grad_reduce = row_contract(active, upstream)
    grad_active = right_contract(upstream, reduce_weight)
    gelu_slope = normal_cdf + hidden_in * jnp.exp(-0.5 * hidden_in * hidden_in) * inv_root_two_pi
    grad_hidden = (grad_active * gelu_slope).astype(bf16)
    grad_expand = row_contract(scaled, grad_hidden)
    grad_scaled = right_contract(grad_hidden, expand_weight) * norm_gain
    grad_field = inverse_spread * (
        grad_scaled
        - jnp.mean(grad_scaled, axis=1, keepdims=True)
        - normed * jnp.mean(grad_scaled * normed, axis=1, keepdims=True)
    )
    grad_field = grad_field.astype(bf16).reshape(row_count, col_count, channels)
    return (
        result.reshape(row_count, col_count, channels),
        upstream.reshape(row_count, col_count, channels),
        grad_field,
        grad_expand,
        grad_reduce,
    )


def block_layout(tile_block, onehot):
    tile_side = tile_block.shape[1]
    placed = jnp.einsum(
        "jp,jxyc->pxyc", onehot, tile_block, preferred_element_type=f32
    ).astype(bf16)
    placed = placed.reshape(2, 2, tile_side, tile_side, -1).transpose(0, 2, 1, 3, 4)
    return placed.reshape(2 * tile_side, 2 * tile_side, -1)


def slot_layout(canvas, onehot):
    tile_side = canvas.shape[0] // 2
    blocks = (
        canvas.reshape(2, tile_side, 2, tile_side, -1)
        .transpose(0, 2, 1, 3, 4)
        .reshape(4, tile_side, tile_side, -1)
    )
    return jnp.einsum("jp,pxyc->jxyc", onehot.astype(f32), blocks, preferred_element_type=f32)


def with_rims(canvas):
    core = lax.axis_index("core")
    upper = lax.axis_index("x") // 2
    strips = canvas.transpose(1, 0, 2)
    west_edge, east_edge = strips[:3], strips[-3:]
    inner = swap(jnp.where(core == 0, east_edge, west_edge), "core", 1)
    outer = lax.ppermute(
        jnp.where(core == 0, west_edge, east_edge),
        ("x", "core"),
        [(1, 2), (2, 1), (5, 6), (6, 5)],
    )
    west = jnp.where(core == 0, outer, inner).transpose(1, 0, 2)
    east = jnp.where(core == 0, inner, outer).transpose(1, 0, 2)
    widened = jnp.concatenate([west, canvas, east], axis=1)
    north_edge, south_edge = widened[:3], widened[-3:]
    near = swap(jnp.where(upper == 0, south_edge, north_edge), "x", 2)
    pairs = [(4 * y + x, 4 * (y + 1) + x - 2) for y in range(3) for x in (2, 3)]
    far = lax.ppermute(
        jnp.where(upper == 0, north_edge, south_edge),
        ("y", "x"),
        pairs + [(b, a) for a, b in pairs],
    )
    north = jnp.where(upper == 0, far, near)
    south = jnp.where(upper == 0, near, far)
    return jnp.concatenate([north, widened, south], axis=0)


def gather_weights(expand_weight, reduce_weight):
    core = lax.axis_index("core")
    rows = jnp.where(core == 0, expand_weight.reshape(reduce_weight.shape), reduce_weight)
    held = rows[None]
    for step, bit in enumerate((4, 2, 1)):
        other = swap(held, "rep", bit)
        mine = bit_of("rep", bit)
        lower = jnp.where(mine == 0, held, other)
        higher = jnp.where(mine == 0, other, held)
        held = jnp.stack([lower, higher], axis=1).reshape(2 ** (step + 1), *rows.shape)
    whole = held.reshape(-1, rows.shape[1])
    other = swap(whole, "core", 1)
    expand_full = jnp.where(core == 0, whole, other)
    reduce_full = jnp.where(core == 0, other, whole)
    return expand_full.reshape(-1, expand_weight.shape[1]), reduce_full


def reduce_gradients(grad_expand, grad_reduce, grad_kern):
    core = lax.axis_index("core")
    width = grad_reduce.shape[1]
    shards = SIZES["rep"]
    expand = grad_expand.astype(bf16).reshape(-1, width)
    project = grad_reduce.astype(bf16)
    rows = expand.shape[0]
    taps = grad_kern.reshape(-1, width)
    tap_count = taps.shape[0]
    taps = jnp.pad(taps, ((0, 64 - tap_count), (0, 0))).astype(bf16)

    def exchange(keep, send, taps, axis, bit):
        got = swap(jnp.concatenate([send, taps], axis=0), axis, bit)
        count = send.shape[0]
        keep = keep.astype(f32) + got[:count].astype(f32)
        taps = (taps.astype(f32) + got[count:].astype(f32)).astype(bf16)
        return keep.astype(bf16), taps

    keep = jnp.where(core == 0, expand, project)
    send = jnp.where(core == 0, project, expand)
    held, taps = exchange(keep, send, taps, "core", 1)
    piece = rows // shards
    for bit in (1, 2, 4):
        parts = held.reshape(-1, 2, piece, width)
        mine = bit_of("rep", bit)
        keep = jnp.where(mine == 0, parts[:, 0], parts[:, 1]).reshape(-1, width)
        send = jnp.where(mine == 0, parts[:, 1], parts[:, 0]).reshape(-1, width)
        held, taps = exchange(keep, send, taps, "rep", bit)
    for axis in ("x", "y"):
        for bit in (1, 2):
            held, taps = exchange(held, held, taps, axis, bit)
    other = swap(held, "core", 1)
    expand = jnp.where(core == 0, held, other).astype(f32)
    project = jnp.where(core == 0, other, held).astype(f32)
    return (
        expand.reshape(-1, grad_expand.shape[1]),
        project,
        taps[:tap_count].astype(f32).reshape(grad_kern.shape),
    )


def per_device(
    tile_data,
    cotangent,
    tile_place,
    tile_count,
    kernel,
    norm_gain,
    expand_weight,
    hidden_bias,
    reduce_weight,
):
    expand_full, reduce_full = gather_weights(expand_weight, reduce_weight)
    slot_count = tile_place.shape[2]
    tile_side = tile_data.shape[2]
    positions = jnp.arange(slot_count)
    live_slots = (positions < tile_count[0, 0]).astype(jnp.int32)
    onehot = (
        (tile_place[0, 0][:, None] == positions[None, :]).astype(jnp.int32) * live_slots[:, None]
    ).astype(bf16)
    canvas = block_layout(tile_data[0], onehot)
    cotan_canvas = block_layout(cotangent[0], onehot)
    live_mask = block_layout(jnp.ones((slot_count, tile_side, tile_side, 1), bf16), onehot)
    padded = with_rims(canvas)
    result, upstream, grad_field, grad_expand, grad_reduce = forward_backward(
        padded, live_mask, cotan_canvas, kernel, norm_gain, expand_full, hidden_bias, reduce_full
    )
    grad_padded = with_rims(grad_field)
    grad_canvas = upstream.astype(f32) + depthwise(grad_padded.astype(f32), kernel[::-1, ::-1])
    grad_canvas = grad_canvas * live_mask.astype(f32)
    grad_kern = depthwise(padded.astype(f32), grad_field.astype(f32))
    sums = reduce_gradients(grad_expand, grad_reduce, grad_kern)
    factor = 1.0 / math.sqrt(SIZES["rep"] * 32 * slot_count * tile_side * tile_side)
    return (
        slot_layout(result, onehot)[None],
        slot_layout(grad_canvas, onehot)[None],
        sums[0] * factor,
        sums[1] * factor,
        sums[2] * factor,
    )


def solution(mesh):
    fine = Mesh(mesh.devices.reshape(4, 4, 2, 8), ("y", "x", "core", "rep"))
    placed = (
        P("rep", TILE, None, None, None),
        P("rep", TILE, None, None, None),
        P("rep", TILE, None),
        P("rep", TILE),
        P(),
        P(),
        P("rep", None),
        P(),
        P("rep", None),
    )
    return jax.shard_map(
        per_device,
        mesh=fine,
        in_specs=placed,
        out_specs=(
            P("rep", TILE, None, None, None),
            P("rep", TILE, None, None, None),
            P("rep", None),
            P("rep", None),
            P(),
        ),
        check_vma=False,
    )
```

```python
import functools

import jax
import jax.numpy as jnp
from jax import lax
from jax.experimental import pallas as pl
from jax.experimental.pallas import tpu as pltpu
from jax.sharding import Mesh, PartitionSpec as P

inv_root_two = 0.7071067811865476
inv_root_two_pi = 0.3989422804014327
bf16 = jnp.bfloat16
f32 = jnp.float32
TILE = ("y", "x", "core")
SIZES = {"y": 4, "x": 4, "core": 2, "rep": 8}
C, FF, S, CAP, KS = 192, 768, 16, 4, 7
SIDE = 2 * S
TAPS = KS * KS
HALF = S + 6
WIDE = SIDE + 8
LANES = 128
TAIL = C - LANES
SHARD = C * FF // SIZES["rep"] // LANES
ROWS = SHARD * SIZES["rep"]
EROWS = C // SIZES["rep"]
RROWS = FF // SIZES["rep"]
GROWS = 48
FACTOR = 1.0 / 512.0
VMEM_LIMIT = 48 * 1024 * 1024


def swap(value, axis, bit):
    return lax.ppermute(value, axis, [(i, i ^ bit) for i in range(SIZES[axis])])


def bit_of(axis, bit):
    return (lax.axis_index(axis) // bit) % 2


def dot(left, right, contract):
    return lax.dot_general(left, right, ((contract[:1], contract[1:]), ((), ())), preferred_element_type=f32)


def place_kernel(place, count, tiles, canvas):
    canvas[...] = jnp.zeros_like(canvas)

    def body(j, carry):
        p = place[0, j]
        row = pl.multiple_of((p // 2) * S, S)
        col = pl.multiple_of((p % 2) * S, S)
        canvas[pl.ds(row, S), pl.ds(col, S), :] = tiles[j]
        return carry

    lax.fori_loop(0, count[0, 0], body, 0)


def fill_planes(padded, planes):
    planes[0] = padded[:HALF, :, :LANES]
    planes[2] = padded[S:, :, :LANES]
    planes[1] = jnp.concatenate([padded[:HALF, :, LANES:], padded[S:, :, LANES:]], axis=-1)


def conv_planes(planes, taps, out):
    def body(step, carry):
        t = step // 4
        col = pl.multiple_of((step % 4) * 8, 8)
        acc = jnp.zeros((S, 8, LANES), f32)
        for dx in range(KS):
            x = planes[t, :, pl.ds(col, 16), :][:, dx : dx + 8, :]
            for dy in range(KS):
                acc = acc + x[dy : dy + S] * taps[t % 2, dy * KS + dx]
        out[t, :, pl.ds(col, 8), :] = acc
        return carry

    lax.fori_loop(0, 12, body, 0)


def correlate_planes(planes, field, acc):
    acc[...] = jnp.zeros_like(acc)

    def body(step, carry):
        t = step // 4
        col = pl.multiple_of((step % 4) * 8, 8)
        g = field[t, :, pl.ds(col, 8), :]
        for dx in range(KS):
            x = planes[t, :, pl.ds(col, 16), :][:, dx : dx + 8, :]
            for dy in range(KS):
                acc[t, dy * KS + dx] += jnp.sum(x[dy : dy + S] * g, axis=0)
        return carry

    lax.fori_loop(0, 12, body, 0)


def tile_of(planes, p):
    lower = p // 2
    col = pl.multiple_of((p % 2) * S, S)
    main = planes[2 * lower, :, pl.ds(col, S), :].reshape(S * S, LANES)
    tail = planes[1, :, pl.ds(col, S), :].reshape(S * S, LANES)
    tail = jnp.where(lower == 1, pltpu.roll(tail, TAIL, 1), tail)
    return jnp.concatenate([main, tail[:, :TAIL]], axis=1)


def pack_expand(value):
    pieces = []
    for z in range(SIZES["rep"]):
        rows = value[z * EROWS : (z + 1) * EROWS]
        pieces += [rows[:, k * LANES : (k + 1) * LANES] for k in range(FF // LANES)]
    return jnp.concatenate(pieces, axis=0)


def pack_reduce(value):
    pieces = []
    for z in range(SIZES["rep"]):
        rows = value[z * RROWS : (z + 1) * RROWS]
        half = RROWS // 2
        pieces.append(rows[:, :LANES])
        pieces.append(jnp.concatenate([rows[:half, LANES:], rows[half:, LANES:]], axis=1))
    return jnp.concatenate(pieces, axis=0)


def unpack_expand(value):
    bands = []
    for z in range(value.shape[0] // SHARD):
        start = z * SHARD
        bands.append(
            jnp.concatenate(
                [value[start + k * EROWS : start + (k + 1) * EROWS] for k in range(FF // LANES)], axis=1
            )
        )
    return jnp.concatenate(bands, axis=0)


def unpack_reduce(value):
    bands = []
    for z in range(value.shape[0] // SHARD):
        start = z * SHARD
        tail = value[start + RROWS : start + SHARD]
        tails = jnp.concatenate([tail[:, :TAIL], tail[:, TAIL:]], axis=0)
        bands.append(jnp.concatenate([value[start : start + RROWS], tails], axis=1))
    return jnp.concatenate(bands, axis=0)


def split_high_low(value):
    high = value.astype(bf16)
    return high, (value - high.astype(f32)).astype(bf16)


def block_kernel(
    place, count, core, padded, tiles, cotan, taps, gain, bias, held, other,
    result, field_out, keep, send, keep_taps,
    planes, filtered, field, tap_acc, expand, project, hidden, active, grad_hidden, grad_e, grad_r,
):
    me = core[0, 0]
    fill_planes(padded, planes)
    conv_planes(planes, taps, filtered)
    mine, theirs = held[...].astype(f32), other[...].astype(f32)
    expand[...] = unpack_expand(jnp.where(me == 0, mine, theirs)).astype(bf16)
    project[...] = unpack_reduce(jnp.where(me == 0, theirs, mine)).astype(bf16)
    field[...] = jnp.zeros_like(field)
    field_out[...] = jnp.zeros_like(field_out)
    grad_e[...] = jnp.zeros_like(grad_e)
    grad_r[...] = jnp.zeros_like(grad_r)

    def blank(j, carry):
        result[j] = jnp.zeros_like(result[j])
        return carry

    lax.fori_loop(count[0, 0], CAP, blank, 0)

    def slot(j, carry):
        p = place[0, j]
        lower = p // 2
        row = pl.multiple_of(lower * S, S)
        col = pl.multiple_of((p % 2) * S, S)
        x = tile_of(filtered, p)
        spread = x - jnp.sum(x, axis=1, keepdims=True) * (1.0 / C)
        inverse = lax.rsqrt(jnp.sum(spread * spread, axis=1, keepdims=True) * (1.0 / C) + 1e-6)
        normed = spread * inverse
        scaled = (normed * gain[...]).astype(bf16)
        up = cotan[j].reshape(S * S, C)
        hidden[0] = dot(scaled, expand[...], (1, 0))
        hidden[1] = dot(up, project[...], (1, 1))

        def gelu(r, carry):
            rows = pl.ds(pl.multiple_of(r * 16, 16), 16)
            h = hidden[0, rows, :] + bias[...]
            cdf = 0.5 * (1.0 + lax.erf(h * inv_root_two))
            slope = cdf + h * jnp.exp(-0.5 * h * h) * inv_root_two_pi
            active[rows, :] = (h * cdf).astype(bf16)
            grad_hidden[rows, :] = (hidden[1, rows, :] * slope).astype(bf16)
            return carry

        lax.fori_loop(0, S, gelu, 0)
        a, gh = active[...], grad_hidden[...]
        mixed = dot(a, project[...], (1, 0))
        result[j] = tiles[j].astype(f32) + mixed.reshape(S, S, C)
        grad_e[...] += dot(scaled, gh, (0, 0))
        grad_r[...] += dot(up, a, (0, 0))
        q = dot(gh, expand[...], (1, 1)) * gain[...]
        mean_q = jnp.sum(q, axis=1, keepdims=True) * (1.0 / C)
        mean_qn = jnp.sum(q * normed, axis=1, keepdims=True) * (1.0 / C)
        g = (inverse * (q - mean_q - normed * mean_qn)).astype(bf16)
        field_out[pl.ds(row, S), pl.ds(col, S), :] = g.reshape(S, S, C)
        g = g.astype(f32)
        field[2 * lower, :, pl.ds(col, S), :] = g[:, :LANES].reshape(S, S, LANES)
        tail = jnp.concatenate([g[:, LANES:], g[:, LANES:]], axis=1).reshape(S, S, LANES)
        old = field[1, :, pl.ds(col, S), :]
        side = lax.broadcasted_iota(jnp.int32, (S, S, LANES), 2) // TAIL
        field[1, :, pl.ds(col, S), :] = jnp.where(side == lower, tail, old)
        return carry

    lax.fori_loop(0, count[0, 0], slot, 0)

    correlate_planes(planes, field, tap_acc)
    sums = jnp.sum(tap_acc[...], axis=2)
    main = sums[0] + sums[2]
    tail = sums[1] + pltpu.roll(sums[1], TAIL, 1)
    pad = jnp.zeros((7, LANES), f32)
    main = jnp.concatenate([main, pad], axis=0)
    tail = jnp.concatenate([tail, pad], axis=0)
    low_lane = lax.broadcasted_iota(jnp.int32, (16, LANES), 1) < TAIL
    halves = []
    for h in range(2):
        s = 24 * h
        tails = jnp.where(low_lane, tail[s : s + 16], tail[s + 16 : s + 32])
        halves.append(jnp.concatenate([main[s : s + 32], tails], axis=0))
    keep_taps[...] = jnp.where(me == 0, halves[0], halves[1])
    high, low = split_high_low(jnp.where(me == 0, halves[1], halves[0]))
    send[ROWS : ROWS + GROWS] = high
    send[ROWS + GROWS :] = low
    e = pack_expand(grad_e[...])
    r = pack_reduce(grad_r[...].T)
    keep[...] = jnp.where(me == 0, e, r).astype(bf16)
    send[:ROWS] = jnp.where(me == 0, r, e).astype(bf16)


def spread_kernel(place, count, padded, cotan, taps, out, planes, summed):
    fill_planes(padded, planes)
    conv_planes(planes, taps, summed)

    def blank(j, carry):
        out[j] = jnp.zeros_like(out[j])
        return carry

    lax.fori_loop(count[0, 0], CAP, blank, 0)

    def slot(j, carry):
        out[j] = cotan[j].astype(f32) + tile_of(summed, place[0, j]).reshape(S, S, C)
        return carry

    lax.fori_loop(0, count[0, 0], slot, 0)


def call(kernel, ins, outs, scratch=(), name=None):
    smem = pl.BlockSpec(memory_space=pltpu.SMEM)
    vmem = pl.BlockSpec(memory_space=pltpu.VMEM)
    specs = [smem if v.dtype == jnp.int32 else vmem for v in ins]
    return pl.pallas_call(
        kernel,
        out_shape=[jax.ShapeDtypeStruct(shape, dtype) for shape, dtype in outs],
        in_specs=specs,
        out_specs=[vmem for _ in outs],
        scratch_shapes=[pltpu.VMEM(shape, dtype) for shape, dtype in scratch],
        compiler_params=pltpu.CompilerParams(vmem_limit_bytes=VMEM_LIMIT),
        name=name,
    )(*ins)


def spread_taps(kernel):
    flat = kernel.reshape(TAPS, C)
    both = jnp.stack([flat[:, :LANES], jnp.concatenate([flat[:, LANES:], flat[:, LANES:]], axis=1)])
    return jnp.broadcast_to(both[:, :, None, :], (2, TAPS, 8, LANES))


def with_rims(canvas):
    core = lax.axis_index("core")
    upper = lax.axis_index("x") // 2
    west_edge = canvas[:, :3].transpose(1, 0, 2)
    east_edge = canvas[:, -3:].transpose(1, 0, 2)
    inner = swap(jnp.where(core == 0, east_edge, west_edge), "core", 1)
    outer = lax.ppermute(
        jnp.where(core == 0, west_edge, east_edge),
        ("x", "core"),
        [(1, 2), (2, 1), (5, 6), (6, 5)],
    )
    west = jnp.where(core == 0, outer, inner).transpose(1, 0, 2)
    east = jnp.where(core == 0, inner, outer).transpose(1, 0, 2)
    blank = jnp.zeros((SIDE, WIDE - SIDE - 6, C), canvas.dtype)
    widened = jnp.concatenate([west, canvas, east, blank], axis=1)
    north_edge, south_edge = widened[:3], widened[-3:]
    near = swap(jnp.where(upper == 0, south_edge, north_edge), "x", 2)
    pairs = [(4 * y + x, 4 * (y + 1) + x - 2) for y in range(3) for x in (2, 3)]
    far = lax.ppermute(
        jnp.where(upper == 0, north_edge, south_edge),
        ("y", "x"),
        pairs + [(b, a) for a, b in pairs],
    )
    north = jnp.where(upper == 0, far, near)
    south = jnp.where(upper == 0, near, far)
    return jnp.concatenate([north, widened, south], axis=0).astype(f32)


def gather_weights(expand_weight, reduce_weight):
    core = lax.axis_index("core")
    half = RROWS // 2
    expand = jnp.concatenate(
        [expand_weight[:, k * LANES : (k + 1) * LANES] for k in range(FF // LANES)], axis=0
    )
    tails = jnp.concatenate([reduce_weight[:half, LANES:], reduce_weight[half:, LANES:]], axis=1)
    project = jnp.concatenate([reduce_weight[:, :LANES], tails], axis=0)
    held = jnp.where(core == 0, expand, project)[None]
    for step, bit in enumerate((4, 2, 1)):
        other = swap(held, "rep", bit)
        mine = bit_of("rep", bit)
        lower = jnp.where(mine == 0, held, other)
        higher = jnp.where(mine == 0, other, held)
        held = jnp.stack([lower, higher], axis=1).reshape(2 ** (step + 1), SHARD, LANES)
    held = held.reshape(ROWS, LANES)
    return held, swap(held, "core", 1)


def reduce_gradients(keep, send, taps):
    got = swap(send, "core", 1)
    held = keep.astype(f32) + got[:ROWS].astype(f32)
    taps = taps + (got[ROWS : ROWS + GROWS].astype(f32) + got[ROWS + GROWS :].astype(f32))
    for bit in (1, 2, 4):
        parts = held.reshape(-1, 2, SHARD, LANES)
        mine = bit_of("rep", bit)
        keep = jnp.where(mine == 0, parts[:, 0], parts[:, 1]).reshape(-1, LANES)
        send = jnp.where(mine == 0, parts[:, 1], parts[:, 0]).reshape(-1, LANES).astype(bf16)
        high, low = split_high_low(taps)
        got = swap(jnp.concatenate([send, high, low], axis=0), "rep", bit)
        count = send.shape[0]
        held = keep + got[:count].astype(f32)
        taps = (high.astype(f32) + low.astype(f32)) + (
            got[count : count + GROWS].astype(f32) + got[count + GROWS :].astype(f32)
        )
    held = jnp.concatenate([held, taps], axis=0)
    for axis in ("x", "y"):
        for bit in (1, 2):
            held = held + swap(held, axis, bit)
    return held * FACTOR


def per_device(
    tile_data,
    cotangent,
    tile_place,
    tile_count,
    kernel,
    norm_gain,
    expand_weight,
    hidden_bias,
    reduce_weight,
):
    core = lax.axis_index("core")
    held, other = gather_weights(expand_weight, reduce_weight)
    tiles, cotan, place = tile_data[0], cotangent[0], tile_place[0]
    (canvas,) = call(place_kernel, (place, tile_count, tiles), [((SIDE, SIDE, C), bf16)], name="place")
    padded = with_rims(canvas)
    plane_shape, cell_shape = (3, HALF, WIDE, LANES), (3, S, SIDE, LANES)
    result, field, keep, send, taps = call(
        block_kernel,
        (
            place,
            tile_count,
            core.reshape(1, 1).astype(jnp.int32),
            padded,
            tiles,
            cotan,
            spread_taps(kernel),
            norm_gain.reshape(1, C),
            hidden_bias.reshape(1, FF),
            held,
            other,
        ),
        [
            ((CAP, S, S, C), f32),
            ((SIDE, SIDE, C), bf16),
            ((ROWS, LANES), bf16),
            ((ROWS + 2 * GROWS, LANES), bf16),
            ((GROWS, LANES), f32),
        ],
        [
            (plane_shape, f32),
            (cell_shape, f32),
            (cell_shape, f32),
            ((3, TAPS, 8, LANES), f32),
            ((C, FF), bf16),
            ((FF, C), bf16),
            ((2, S * S, FF), f32),
            ((S * S, FF), bf16),
            ((S * S, FF), bf16),
            ((C, FF), f32),
            ((C, FF), f32),
        ],
        name="block",
    )
    (grad_tiles,) = call(
        spread_kernel,
        (place, tile_count, with_rims(field), cotan, spread_taps(kernel[::-1, ::-1])),
        [((CAP, S, S, C), f32)],
        [(plane_shape, f32), (cell_shape, f32)],
        name="spread",
    )
    held = reduce_gradients(keep, send, taps)
    other = swap(held, "core", 1)
    first = jnp.where(core == 0, held, other)
    second = jnp.where(core == 0, other, held)
    halves = []
    for half in (first[SHARD:], second[SHARD:]):
        tails = jnp.concatenate([half[32:48, :TAIL], half[32:48, TAIL:]], axis=0)
        halves.append(jnp.concatenate([half[:32], tails], axis=1))
    grad_kernel = jnp.concatenate([halves[0][:24], halves[1][:25]], axis=0)
    return (
        result[None],
        grad_tiles[None],
        unpack_expand(first[:SHARD]),
        unpack_reduce(second[:SHARD]),
        grad_kernel.reshape(KS, KS, C),
    )


def solution(mesh):
    fine = Mesh(mesh.devices.reshape(4, 4, 2, 8), ("y", "x", "core", "rep"))
    tiles = P("rep", TILE, None, None, None)
    placed = (
        tiles,
        tiles,
        P("rep", TILE, None),
        P("rep", TILE),
        P(),
        P(),
        P("rep", None),
        P(),
        P("rep", None),
    )
    return jax.shard_map(
        per_device,
        mesh=fine,
        in_specs=placed,
        out_specs=(tiles, tiles, P("rep", None), P("rep", None), P()),
        check_vma=False,
    )
```

```python
import functools

import jax
import jax.numpy as jnp
from jax import lax
from jax.experimental import pallas as pl
from jax.experimental.pallas import tpu as pltpu
from jax.sharding import Mesh, PartitionSpec as P

inv_root_two = 0.7071067811865476
inv_root_two_pi = 0.3989422804014327
bf16 = jnp.bfloat16
f32 = jnp.float32
REP_ORDER = (0, 2, 4, 6, 1, 3, 5, 7)
TILE = ("y", "x", "core")
SIZES = {"y": 4, "x": 4, "core": 2, "rep": 8}
C, FF, S, CAP, KS = 192, 768, 16, 4, 7
SIDE = 2 * S
TAPS = KS * KS
HALF = S + 6
WIDE = SIDE + 8
LANES = 128
TAIL = C - LANES
SHARD = C * FF // SIZES["rep"] // LANES
ROWS = SHARD * SIZES["rep"]
EROWS = C // SIZES["rep"]
RROWS = FF // SIZES["rep"]
CHUNK = 40
GROWS = 64
PIECE = GROWS // 4
PART = CHUNK + PIECE
FACTOR = 1.0 / 512.0
VMEM_LIMIT = 48 * 1024 * 1024


def swap(value, axis, bit):
    return lax.ppermute(value, axis, [(i, i ^ bit) for i in range(SIZES[axis])])


def bit_of(axis, bit):
    return (lax.axis_index(axis) // bit) % 2


def dot(left, right, contract):
    return lax.dot_general(left, right, ((contract[:1], contract[1:]), ((), ())), preferred_element_type=f32)


CORE, AT_X, AT_REP, COUNT, PLACE = 0, 1, 2, 3, 4


def place_kernel(info, tiles, expand, project, canvas, packed, held_e, held_r, sems, tile_sems):
    weights = [
        pltpu.make_async_copy(expand, held_e, sems.at[0]),
        pltpu.make_async_copy(project, held_r, sems.at[1]),
    ]
    for copy in weights:
        copy.start()

    def tile_copy(j):
        p = info[0, PLACE + j]
        row = pl.multiple_of((p // 2) * S, S)
        col = pl.multiple_of((p % 2) * S, S)
        return row, col, pltpu.make_async_copy(
            tiles.at[j], canvas.at[pl.ds(row, S), pl.ds(col, S), :], tile_sems.at[j]
        )

    for j in range(CAP):
        row, col, copy = tile_copy(j)

        @pl.when(j < info[0, COUNT])
        def _():
            copy.start()

        @pl.when(j >= info[0, COUNT])
        def _():
            canvas[pl.ds(row, S), pl.ds(col, S), :] = jnp.zeros((S, S, C), bf16)

    for copy in weights:
        copy.wait()
    e, r = pack_expand(held_e[...].astype(f32)), pack_reduce(held_r[...].astype(f32))
    packed[...] = jnp.where(info[0, CORE] == 0, e, r).astype(bf16)
    for j in range(CAP):

        @pl.when(j < info[0, COUNT])
        def _():
            tile_copy(j)[2].wait()


def fill_taps(kernel, taps, flip):
    for dy in range(KS):
        for dx in range(KS):
            row = kernel[KS - 1 - dy, KS - 1 - dx : KS - dx] if flip else kernel[dy, dx : dx + 1]
            both = jnp.concatenate([row[:, LANES:], row[:, LANES:]], axis=1)
            taps[0, dy * KS + dx] = jnp.broadcast_to(row[:, :LANES], (8, LANES))
            taps[1, dy * KS + dx] = jnp.broadcast_to(both, (8, LANES))


def field_kernel(padded, kernel, planes, filtered, taps):
    fill_taps(kernel, taps, False)
    fill_planes(padded, planes)
    conv_planes(planes, taps, filtered)


def fill_planes(padded, planes):
    planes[0] = padded[:HALF, :, :LANES]
    planes[2] = padded[S:, :, :LANES]
    planes[1] = jnp.concatenate([padded[:HALF, :, LANES:], padded[S:, :, LANES:]], axis=-1)


def conv_planes(planes, taps, out):
    def body(step, carry):
        t = step // 4
        col = pl.multiple_of((step % 4) * 8, 8)
        acc = jnp.zeros((S, 8, LANES), f32)
        for dx in range(KS):
            x = planes[t, :, pl.ds(col + dx, 8), :]
            for dy in range(KS):
                acc = acc + x[dy : dy + S] * taps[t % 2, dy * KS + dx]
        out[t, :, pl.ds(col, 8), :] = acc
        return carry

    lax.fori_loop(0, 12, body, 0)


def correlate_planes(planes, field, acc):
    acc[...] = jnp.zeros_like(acc)

    def body(step, carry):
        t = step // 4
        col = pl.multiple_of((step % 4) * 8, 8)
        g = [field[t, row, pl.ds(col, 8), :] for row in range(S)]
        for dx in range(KS):
            sums = [None] * KS
            for row in range(HALF):
                x = planes[t, row, pl.ds(col + dx, 8), :]
                for dy in range(max(0, row - S + 1), min(KS, row + 1)):
                    term = x * g[row - dy]
                    sums[dy] = term if sums[dy] is None else sums[dy] + term
            for dy in range(KS):
                acc[t, dy * KS + dx] += sums[dy]
        return carry

    lax.fori_loop(0, 12, body, 0)


def tile_of(planes, p):
    lower = p // 2
    col = pl.multiple_of((p % 2) * S, S)
    main = planes[2 * lower, :, pl.ds(col, S), :].reshape(S * S, LANES)
    tail = planes[1, :, pl.ds(col, S), :].reshape(S * S, LANES)
    tail = jnp.where(lower == 1, pltpu.roll(tail, TAIL, 1), tail)
    return jnp.concatenate([main, tail[:, :TAIL]], axis=1)


def pack_expand(rows):
    return jnp.concatenate([rows[:, k * LANES : (k + 1) * LANES] for k in range(FF // LANES)], axis=0)


def pack_reduce(rows):
    half = RROWS // 2
    tails = jnp.concatenate([rows[:half, LANES:], rows[half:, LANES:]], axis=1)
    return jnp.concatenate([rows[:, :LANES], tails], axis=0)


def unpack_expand(value):
    return jnp.concatenate([value[k * EROWS : (k + 1) * EROWS] for k in range(FF // LANES)], axis=1)


def unpack_reduce(value):
    tail = value[RROWS:SHARD]
    tails = jnp.concatenate([tail[:, :TAIL], tail[:, TAIL:]], axis=0)
    return jnp.concatenate([value[:RROWS], tails], axis=1)


def split_high_low(value):
    high = value.astype(bf16)
    return high, (value - high.astype(f32)).astype(bf16)


def block_kernel(
    info, planes, filtered, tiles, cotan, gain, bias, held, other,
    result, field_out, keep, send, keep_taps,
    field, tap_acc, expand_wide, expand, project, hidden, active, grad_hidden,
    grad_e, grad_r, grad_rt, shards, tap_rows,
):
    me, my_x, my_z = info[0, CORE], info[0, AT_X], info[0, AT_REP]
    for k, s in enumerate(REP_ORDER):
        z = my_z ^ s
        mine, theirs = held[k].astype(f32), other[k].astype(f32)
        rows = pl.ds(pl.multiple_of(z * EROWS, 8), EROWS)
        expand_wide[rows, :] = unpack_expand(jnp.where(me == 0, mine, theirs))
        rows = pl.ds(pl.multiple_of(z * RROWS, RROWS), RROWS)
        project[rows, :] = unpack_reduce(jnp.where(me == 0, theirs, mine)).astype(bf16)
    expand[...] = expand_wide[...].astype(bf16)
    field[...] = jnp.zeros_like(field)
    field_out[...] = jnp.zeros_like(field_out)
    grad_e[...] = jnp.zeros_like(grad_e)
    grad_r[...] = jnp.zeros_like(grad_r)

    def blank(j, carry):
        result[j] = jnp.zeros_like(result[j])
        return carry

    lax.fori_loop(info[0, COUNT], CAP, blank, 0)

    def slot(j, carry):
        p = info[0, PLACE + j]
        lower = p // 2
        row = pl.multiple_of(lower * S, S)
        col = pl.multiple_of((p % 2) * S, S)
        x = tile_of(filtered, p)
        spread = x - jnp.sum(x, axis=1, keepdims=True) * (1.0 / C)
        inverse = lax.rsqrt(jnp.sum(spread * spread, axis=1, keepdims=True) * (1.0 / C) + 1e-6)
        normed = spread * inverse
        scaled = (normed * gain[...]).astype(bf16)
        up = cotan[j].reshape(S * S, C)
        hidden[0] = dot(scaled, expand[...], (1, 0))
        hidden[1] = dot(up, project[...], (1, 1))

        def gelu(r, carry):
            rows = pl.ds(pl.multiple_of(r * 16, 16), 16)
            h = hidden[0, rows, :] + bias[...]
            cdf = 0.5 * (1.0 + lax.erf(h * inv_root_two))
            slope = cdf + h * jnp.exp(-0.5 * h * h) * inv_root_two_pi
            active[rows, :] = (h * cdf).astype(bf16)
            grad_hidden[rows, :] = (hidden[1, rows, :] * slope).astype(bf16)
            return carry

        lax.fori_loop(0, S, gelu, 0)
        a, gh = active[...], grad_hidden[...]
        mixed = dot(a, project[...], (1, 0))
        result[j] = tiles[j].astype(f32) + mixed.reshape(S, S, C)
        grad_e[...] += dot(scaled, gh, (0, 0))
        grad_r[...] += dot(up, a, (0, 0))
        q = dot(gh, expand[...], (1, 1)) * gain[...]
        mean_q = jnp.sum(q, axis=1, keepdims=True) * (1.0 / C)
        mean_qn = jnp.sum(q * normed, axis=1, keepdims=True) * (1.0 / C)
        g = (inverse * (q - mean_q - normed * mean_qn)).astype(bf16)
        field_out[pl.ds(row, S), pl.ds(col, S), :] = g.reshape(S, S, C)
        g = g.astype(f32)
        field[2 * lower, :, pl.ds(col, S), :] = g[:, :LANES].reshape(S, S, LANES)
        tail = jnp.concatenate([g[:, LANES:], g[:, LANES:]], axis=1).reshape(S, S, LANES)
        old = field[1, :, pl.ds(col, S), :]
        side = lax.broadcasted_iota(jnp.int32, (S, S, LANES), 2) // TAIL
        field[1, :, pl.ds(col, S), :] = jnp.where(side == lower, tail, old)
        return carry

    lax.fori_loop(0, info[0, COUNT], slot, 0)

    correlate_planes(planes, field, tap_acc)
    sums = jnp.sum(tap_acc[...], axis=2)
    main = sums[0] + sums[2]
    tail = sums[1] + pltpu.roll(sums[1], TAIL, 1)
    pad = jnp.zeros((7, LANES), f32)
    main = jnp.concatenate([main, pad], axis=0)
    tail = jnp.concatenate([tail, pad], axis=0)
    low_lane = lax.broadcasted_iota(jnp.int32, (16, LANES), 1) < TAIL
    for h in range(2):
        s = 24 * h
        tails = jnp.where(low_lane, tail[s : s + 16], tail[s + 16 : s + 32])
        tap_rows[h] = jnp.concatenate([main[s : s + 32], tails, jnp.zeros((16, LANES), f32)], axis=0)
    for i in range(4):
        rows = pl.ds(pl.multiple_of((my_x ^ i) * PIECE, PIECE), PIECE)
        keep_taps[i] = tap_rows[me, rows, :]
        high, low = split_high_low(tap_rows[1 - me, rows, :])
        send[i, 8 * CHUNK : 8 * CHUNK + PIECE] = high
        send[i, 8 * CHUNK + PIECE :] = low
    grad_rt[...] = grad_r[...].T
    shards[:, SHARD:] = jnp.zeros((2, 4 * CHUNK - SHARD, LANES), f32)
    for k in range(8):
        z = my_z ^ k
        e = pack_expand(grad_e[pl.ds(pl.multiple_of(z * EROWS, 8), EROWS), :])
        r = pack_reduce(grad_rt[pl.ds(pl.multiple_of(z * RROWS, RROWS), RROWS), :])
        shards[0, :SHARD] = jnp.where(me == 0, e, r)
        shards[1, :SHARD] = jnp.where(me == 0, r, e)
        for i in range(4):
            rows = pl.ds(pl.multiple_of((my_x ^ i) * CHUNK, 8), CHUNK)
            keep[i, k * CHUNK : (k + 1) * CHUNK] = shards[0, rows, :]
            send[i, k * CHUNK : (k + 1) * CHUNK] = shards[1, rows, :].astype(bf16)


def finish_kernel(info, held, other, grad_e, grad_r, grad_k, shards, tap_rows):
    me, my_x = info[0, CORE], info[0, AT_X]
    for i in range(4):
        rows = pl.ds(pl.multiple_of((my_x ^ i) * CHUNK, 8), CHUNK)
        taps = pl.ds(pl.multiple_of((my_x ^ i) * PIECE, PIECE), PIECE)
        shards[me, rows, :] = held[i, :CHUNK]
        shards[1 - me, rows, :] = other[i, :CHUNK]
        tap_rows[me, taps, :] = held[i, CHUNK:]
        tap_rows[1 - me, taps, :] = other[i, CHUNK:]
    grad_e[...] = unpack_expand(shards[0]) * FACTOR
    grad_r[...] = unpack_reduce(shards[1]) * FACTOR
    halves = []
    for h in range(2):
        half = tap_rows[h]
        tails = jnp.concatenate([half[32:48, :TAIL], half[32:48, TAIL:]], axis=0)
        halves.append(jnp.concatenate([half[:32], tails], axis=1))
    whole = jnp.concatenate([halves[0][:24], halves[1]], axis=0) * FACTOR
    for dy in range(KS):
        grad_k[dy] = whole[dy * KS : (dy + 1) * KS]


def spread_kernel(info, padded, cotan, kernel, out, planes, summed, taps):
    fill_taps(kernel, taps, True)
    fill_planes(padded, planes)
    conv_planes(planes, taps, summed)

    def blank(j, carry):
        out[j] = jnp.zeros_like(out[j])
        return carry

    lax.fori_loop(info[0, COUNT], CAP, blank, 0)

    def slot(j, carry):
        out[j] = cotan[j].astype(f32) + tile_of(summed, info[0, PLACE + j]).reshape(S, S, C)
        return carry

    lax.fori_loop(0, info[0, COUNT], slot, 0)


def call(kernel, ins, outs, scratch=(), name=None, hbm=(), us=1):
    smem = pl.BlockSpec(memory_space=pltpu.SMEM)
    vmem = pl.BlockSpec(memory_space=pltpu.VMEM)
    specs = [smem if v.dtype == jnp.int32 else vmem for v in ins]
    for i in hbm:
        specs[i] = pl.BlockSpec(memory_space=pltpu.HBM)
    return pl.pallas_call(
        kernel,
        out_shape=[jax.ShapeDtypeStruct(shape, dtype) for shape, dtype in outs],
        in_specs=specs,
        out_specs=[vmem for _ in outs],
        scratch_shapes=[pltpu.VMEM(*s) if isinstance(s, tuple) else s for s in scratch],
        compiler_params=pltpu.CompilerParams(vmem_limit_bytes=VMEM_LIMIT),
        cost_estimate=pl.CostEstimate(flops=us * 10**9, bytes_accessed=us * 10**6, transcendentals=0),
        name=name,
    )(*ins)


TAP_PLANES = (2, TAPS, 8, LANES)
PLANES, CELLS = (3, HALF, WIDE, LANES), (3, S, SIDE, LANES)


def block_call(*ins):
    return call(
        block_kernel,
        ins,
        [
            ((CAP, S, S, C), f32),
            ((SIDE, SIDE, C), bf16),
            ((4, 8 * CHUNK, LANES), f32),
            ((4, 8 * CHUNK + 2 * PIECE, LANES), bf16),
            ((4, PIECE, LANES), f32),
        ],
        [
            (CELLS, f32),
            ((3, TAPS, 8, LANES), f32),
            ((C, FF), f32),
            ((C, FF), bf16),
            ((FF, C), bf16),
            ((2, S * S, FF), f32),
            ((S * S, FF), bf16),
            ((S * S, FF), bf16),
            ((C, FF), f32),
            ((C, FF), f32),
            ((FF, C), f32),
            ((2, 4 * CHUNK, LANES), f32),
            ((2, GROWS, LANES), f32),
        ],
        name="block",
        us=14,
    )


def side_rims(canvas):
    core = lax.axis_index("core")
    west_edge = canvas[:, :3].transpose(1, 0, 2)
    east_edge = canvas[:, -3:].transpose(1, 0, 2)
    inner = swap(jnp.where(core == 0, east_edge, west_edge), "core", 1)
    pairs = [(4 * i + a, 4 * i + 3 - a) for i in range(2) for a in range(4)]
    outer = lax.ppermute(jnp.where(core == 0, west_edge, east_edge), ("x", "core"), pairs)
    return inner, jnp.where(lax.axis_index("x") % 2 != core, outer, jnp.zeros_like(outer))


def widen(canvas, inner, outer):
    core = lax.axis_index("core")
    west = jnp.where(core == 0, outer, inner).transpose(1, 0, 2)
    east = jnp.where(core == 0, inner, outer).transpose(1, 0, 2)
    blank = jnp.zeros((SIDE, WIDE - SIDE - 6, C), canvas.dtype)
    return jnp.concatenate([west, canvas, east, blank], axis=1)


def end_rims(widened):
    upper = lax.axis_index("x") // 2
    north_edge, south_edge = widened[:3], widened[-3:]
    near = swap(jnp.where(upper == 0, south_edge, north_edge), "x", 2)
    pairs = [(4 * y + x, 4 * ((y + 1) % 4) + x - 2) for y in range(4) for x in (2, 3)]
    far = lax.ppermute(
        jnp.where(upper == 0, north_edge, south_edge),
        ("y", "x"),
        pairs + [(b, a) for a, b in pairs],
    )
    inside = jnp.where(upper == 0, lax.axis_index("y") > 0, lax.axis_index("y") < 3)
    return near, jnp.where(inside, far, jnp.zeros_like(far))


def pad_ends(widened, near, far):
    upper = lax.axis_index("x") // 2
    north = jnp.where(upper == 0, far, near)
    south = jnp.where(upper == 0, near, far)
    return jnp.concatenate([north, widened, south], axis=0).astype(f32)


def tie(value, *others):
    return lax.optimization_barrier((value, *others))


def rows_sum(own, got):
    return (own + got[0]) + (got[1] + got[2])


def join(value):
    return value[..., :PIECE, :].astype(f32) + value[..., PIECE:, :].astype(f32)


def per_device(
    tile_data,
    cotangent,
    tile_place,
    tile_count,
    kernel,
    norm_gain,
    expand_weight,
    hidden_bias,
    reduce_weight,
):
    scalars = [lax.axis_index(a) for a in ("core", "x", "rep")] + [tile_count[0, 0]]
    info = jnp.concatenate([jnp.stack(scalars).astype(jnp.int32), tile_place[0, 0]])[None]
    tiles, cotan = tile_data[0], cotangent[0]
    canvas, packed = call(
        place_kernel,
        (info, tiles, expand_weight, reduce_weight),
        [((SIDE, SIDE, C), bf16), ((SHARD, LANES), bf16)],
        [
            ((EROWS, FF), bf16),
            ((RROWS, C), bf16),
            pltpu.SemaphoreType.DMA((2,)),
            pltpu.SemaphoreType.DMA((CAP,)),
        ],
        name="place",
        hbm=(1, 2, 3),
        us=2,
    )
    inner, outer = side_rims(canvas)
    packed, inner = tie(packed, inner)
    held = jnp.stack([packed] + [swap(packed, "rep", bits) for bits in (2, 4, 6)])
    widened = widen(canvas, inner, outer)
    near, far = end_rims(widened)
    held = jnp.concatenate([held, swap(held, "rep", 1)])
    planes, filtered = call(
        field_kernel,
        (pad_ends(widened, near, far), kernel),
        [(PLANES, f32), (CELLS, f32)],
        [(TAP_PLANES, f32)],
        name="field",
        us=5,
    )
    other = swap(held, "core", 1)
    result, field, keep, send, taps = block_call(
        info,
        planes,
        filtered,
        tiles,
        cotan,
        norm_gain.reshape(1, C),
        hidden_bias.reshape(1, FF),
        held,
        other,
    )
    end, pair = 8 * CHUNK, 2 * CHUNK
    got = swap(send, "core", 1)
    inner, outer = side_rims(field)
    held = keep + got[:, :end].astype(f32)
    taps = taps + join(got[:, end:])
    high, low = split_high_low(taps)
    send = jnp.concatenate([held.astype(bf16), high, low], axis=1)
    got = [swap(send[i], "x", i) for i in (1, 2, 3)]
    widened = widen(field, inner, outer)
    near, far = end_rims(widened)
    held = rows_sum(held[0], [g[:end].astype(f32) for g in got])
    taps = rows_sum(taps[0], [join(g[end:]) for g in got])
    high, low = split_high_low(taps)
    sends = [
        jnp.concatenate([held[k * CHUNK : k * CHUNK + pair].astype(bf16), high, low]) for k in (2, 4, 6)
    ]
    *sends, near, far = tie(*sends, near, far)
    got = [swap(part, "rep", k) for part, k in zip(sends, (2, 4, 6))]
    (grad_tiles,) = call(
        spread_kernel,
        (info, pad_ends(widened, near, far), cotan, kernel),
        [((CAP, S, S, C), f32)],
        [(PLANES, f32), (CELLS, f32), (TAP_PLANES, f32)],
        name="spread",
        us=6,
    )
    held = rows_sum(held[:pair], [g[:pair].astype(f32) for g in got])
    taps = rows_sum(high.astype(f32) + low.astype(f32), [join(g[pair:]) for g in got])
    part, grad_tiles = tie(jnp.concatenate([held[CHUNK:], taps]), grad_tiles)
    held = jnp.concatenate([held[:CHUNK], taps]) + swap(part, "rep", 1)
    held = rows_sum(held, [swap(held, "y", i) for i in (1, 2, 3)])
    held = jnp.stack([held] + [swap(held, "x", i) for i in (1, 2, 3)])
    grad_expand, grad_reduce, grad_kernel = call(
        finish_kernel,
        (info, held, swap(held, "core", 1)),
        [((EROWS, FF), f32), ((RROWS, C), f32), ((KS, KS, C), f32)],
        [((2, 4 * CHUNK, LANES), f32), ((2, GROWS, LANES), f32)],
        name="finish",
    )
    return result[None], grad_tiles[None], grad_expand, grad_reduce, grad_kernel


def solution(mesh):
    fine = Mesh(mesh.devices.reshape(4, 4, 2, 8), ("y", "x", "core", "rep"))
    tiles = P("rep", TILE, None, None, None)
    placed = (
        tiles,
        tiles,
        P("rep", TILE, None),
        P("rep", TILE),
        P(),
        P(),
        P("rep", None),
        P(),
        P("rep", None),
    )
    return jax.shard_map(
        per_device,
        mesh=fine,
        in_specs=placed,
        out_specs=(tiles, tiles, P("rep", None), P("rep", None), P()),
        check_vma=False,
    )
```

```python
import functools

import jax
import jax.numpy as jnp
from jax import lax
from jax.experimental import pallas as pl
from jax.experimental.pallas import tpu as pltpu
from jax.sharding import Mesh, PartitionSpec as P

inv_root_two = 0.7071067811865476
inv_root_two_pi = 0.3989422804014327
bf16 = jnp.bfloat16
f32 = jnp.float32
REP_ORDER = (0, 7, 2, 5, 1, 6, 3, 4)
SUM_ORDER = (0, 2, 1, 3, 6, 4, 7, 5)
TILE = ("y", "x", "core")
SIZES = {"y": 4, "x": 4, "core": 2, "rep": 8}
C, FF, S, CAP, KS = 192, 768, 16, 4, 7
SIDE = 2 * S
TAPS = KS * KS
HALF = S + 6
WIDE = SIDE + 8
LANES = 128
TAIL = C - LANES
SHARD = C * FF // SIZES["rep"] // LANES
ROWS = SHARD * SIZES["rep"]
EROWS = C // SIZES["rep"]
RROWS = FF // SIZES["rep"]
GROWS = 48
FACTOR = 1.0 / 512.0
VMEM_LIMIT = 48 * 1024 * 1024


def swap(value, axis, bit):
    return lax.ppermute(value, axis, [(i, i ^ bit) for i in range(SIZES[axis])])


def bit_of(axis, bit):
    return (lax.axis_index(axis) // bit) % 2


def dot(left, right, contract):
    return lax.dot_general(left, right, ((contract[:1], contract[1:]), ((), ())), preferred_element_type=f32)


CORE, AT_REP, COUNT, PLACE = 0, 1, 2, 3


def place_kernel(info, tiles, canvas, sems):
    def tile_copy(j):
        p = info[0, PLACE + j]
        row = pl.multiple_of((p // 2) * S, S)
        col = pl.multiple_of((p % 2) * S, S)
        return row, col, pltpu.make_async_copy(
            tiles.at[j], canvas.at[pl.ds(row, S), pl.ds(col, S), :], sems.at[j]
        )

    for j in range(CAP):
        row, col, copy = tile_copy(j)

        @pl.when(j < info[0, COUNT])
        def _():
            copy.start()

        @pl.when(j >= info[0, COUNT])
        def _():
            canvas[pl.ds(row, S), pl.ds(col, S), :] = jnp.zeros((S, S, C), bf16)

    for j in range(CAP):

        @pl.when(j < info[0, COUNT])
        def _():
            tile_copy(j)[2].wait()


def pack_kernel(info, expand, project, packed):
    e, r = pack_expand(expand[...].astype(f32)), pack_reduce(project[...].astype(f32))
    packed[...] = jnp.where(info[0, CORE] == 0, e, r).astype(bf16)


def fill_taps(kernel, taps, flip):
    for dy in range(KS):
        for dx in range(KS):
            row = kernel[KS - 1 - dy, KS - 1 - dx : KS - dx] if flip else kernel[dy, dx : dx + 1]
            both = jnp.concatenate([row[:, LANES:], row[:, LANES:]], axis=1)
            taps[0, dy * KS + dx] = jnp.broadcast_to(row[:, :LANES], (8, LANES))
            taps[1, dy * KS + dx] = jnp.broadcast_to(both, (8, LANES))


def field_kernel(padded, kernel, planes, filtered, taps):
    fill_taps(kernel, taps, False)
    fill_planes(padded, planes)
    conv_planes(planes, taps, filtered)


def fill_planes(padded, planes):
    planes[0] = padded[:HALF, :, :LANES]
    planes[2] = padded[S:, :, :LANES]
    planes[1] = jnp.concatenate([padded[:HALF, :, LANES:], padded[S:, :, LANES:]], axis=-1)


def conv_planes(planes, taps, out):
    def body(step, carry):
        t = step // 4
        col = pl.multiple_of((step % 4) * 8, 8)
        acc = jnp.zeros((S, 8, LANES), f32)
        for dx in range(KS):
            x = planes[t, :, pl.ds(col + dx, 8), :]
            for dy in range(KS):
                acc = acc + x[dy : dy + S] * taps[t % 2, dy * KS + dx]
        out[t, :, pl.ds(col, 8), :] = acc
        return carry

    lax.fori_loop(0, 12, body, 0)


def correlate_planes(planes, field, acc):
    acc[...] = jnp.zeros_like(acc)

    def body(step, carry):
        t = step // 4
        col = pl.multiple_of((step % 4) * 8, 8)
        g = [field[t, row, pl.ds(col, 8), :] for row in range(S)]
        for dx in range(KS):
            sums = [None] * KS
            for row in range(HALF):
                x = planes[t, row, pl.ds(col + dx, 8), :]
                for dy in range(max(0, row - S + 1), min(KS, row + 1)):
                    term = x * g[row - dy]
                    sums[dy] = term if sums[dy] is None else sums[dy] + term
            for dy in range(KS):
                acc[t, dy * KS + dx] += sums[dy]
        return carry

    lax.fori_loop(0, 12, body, 0)


def tile_of(planes, p):
    lower = p // 2
    col = pl.multiple_of((p % 2) * S, S)
    main = planes[2 * lower, :, pl.ds(col, S), :].reshape(S * S, LANES)
    tail = planes[1, :, pl.ds(col, S), :].reshape(S * S, LANES)
    tail = jnp.where(lower == 1, pltpu.roll(tail, TAIL, 1), tail)
    return jnp.concatenate([main, tail[:, :TAIL]], axis=1)


def pack_expand(rows):
    return jnp.concatenate([rows[:, k * LANES : (k + 1) * LANES] for k in range(FF // LANES)], axis=0)


def pack_reduce(rows):
    half = RROWS // 2
    tails = jnp.concatenate([rows[:half, LANES:], rows[half:, LANES:]], axis=1)
    return jnp.concatenate([rows[:, :LANES], tails], axis=0)


def unpack_expand(value):
    return jnp.concatenate([value[k * EROWS : (k + 1) * EROWS] for k in range(FF // LANES)], axis=1)


def unpack_reduce(value):
    tail = value[RROWS:SHARD]
    tails = jnp.concatenate([tail[:, :TAIL], tail[:, TAIL:]], axis=0)
    return jnp.concatenate([value[:RROWS], tails], axis=1)


def split_high_low(value):
    high = value.astype(bf16)
    return high, (value - high.astype(f32)).astype(bf16)


def block_kernel(
    info, planes, filtered, tiles, cotan, gain, bias, held, other,
    result, field_out, keep, send, keep_taps,
    field, tap_acc, expand_wide, expand, project, hidden, active, grad_hidden,
    grad_e, grad_r, grad_rt,
):
    me, my_z = info[0, CORE], info[0, AT_REP]
    for k, s in enumerate(REP_ORDER):
        z = my_z ^ s
        mine, theirs = held[k].astype(f32), other[k].astype(f32)
        rows = pl.ds(pl.multiple_of(z * EROWS, 8), EROWS)
        expand_wide[rows, :] = unpack_expand(jnp.where(me == 0, mine, theirs))
        rows = pl.ds(pl.multiple_of(z * RROWS, RROWS), RROWS)
        project[rows, :] = unpack_reduce(jnp.where(me == 0, theirs, mine)).astype(bf16)
    expand[...] = expand_wide[...].astype(bf16)
    field[...] = jnp.zeros_like(field)
    field_out[...] = jnp.zeros_like(field_out)
    grad_e[...] = jnp.zeros_like(grad_e)
    grad_r[...] = jnp.zeros_like(grad_r)

    def slot(j):
        live = j < info[0, COUNT]
        p = info[0, PLACE + j]
        lower = p // 2
        row = pl.multiple_of(lower * S, S)
        col = pl.multiple_of((p % 2) * S, S)
        x = tile_of(filtered, p)
        spread = x - jnp.sum(x, axis=1, keepdims=True) * (1.0 / C)
        inverse = lax.rsqrt(jnp.sum(spread * spread, axis=1, keepdims=True) * (1.0 / C) + 1e-6)
        normed = spread * inverse
        scaled = (normed * gain[...]).astype(bf16)
        up = jnp.where(live, cotan[j].reshape(S * S, C), jnp.zeros((S * S, C), bf16))
        hidden[j, 0] = dot(scaled, expand[...], (1, 0))
        hidden[j, 1] = dot(up, project[...], (1, 1))

        def gelu(r, carry):
            rows = pl.ds(pl.multiple_of(r * 16, 16), 16)
            h = hidden[j, 0, rows, :] + bias[...]
            cdf = 0.5 * (1.0 + lax.erf(h * inv_root_two))
            slope = cdf + h * jnp.exp(-0.5 * h * h) * inv_root_two_pi
            active[j, rows, :] = (h * cdf).astype(bf16)
            grad_hidden[j, rows, :] = (hidden[j, 1, rows, :] * slope).astype(bf16)
            return carry

        lax.fori_loop(0, S, gelu, 0, unroll=S)
        a, gh = active[j], grad_hidden[j]
        mixed = dot(a, project[...], (1, 0))
        result[j] = jnp.where(live, tiles[j].astype(f32) + mixed.reshape(S, S, C), jnp.zeros((S, S, C), f32))
        grad_e[...] += dot(scaled, gh, (0, 0))
        grad_r[...] += dot(up, a, (0, 0))
        q = dot(gh, expand[...], (1, 1)) * gain[...]
        mean_q = jnp.sum(q, axis=1, keepdims=True) * (1.0 / C)
        mean_qn = jnp.sum(q * normed, axis=1, keepdims=True) * (1.0 / C)
        g = (inverse * (q - mean_q - normed * mean_qn)).astype(bf16)
        field_out[pl.ds(row, S), pl.ds(col, S), :] = g.reshape(S, S, C)
        g = g.astype(f32)
        field[2 * lower, :, pl.ds(col, S), :] = g[:, :LANES].reshape(S, S, LANES)
        tail = jnp.concatenate([g[:, LANES:], g[:, LANES:]], axis=1).reshape(S, S, LANES)
        old = field[1, :, pl.ds(col, S), :]
        side = lax.broadcasted_iota(jnp.int32, (S, S, LANES), 2) // TAIL
        field[1, :, pl.ds(col, S), :] = jnp.where(side == lower, tail, old)

    for j in range(CAP):
        slot(j)

    correlate_planes(planes, field, tap_acc)
    sums = jnp.sum(tap_acc[...], axis=2)
    main = sums[0] + sums[2]
    tail = sums[1] + pltpu.roll(sums[1], TAIL, 1)
    pad = jnp.zeros((7, LANES), f32)
    main = jnp.concatenate([main, pad], axis=0)
    tail = jnp.concatenate([tail, pad], axis=0)
    low_lane = lax.broadcasted_iota(jnp.int32, (16, LANES), 1) < TAIL
    halves = []
    for h in range(2):
        s = 24 * h
        tails = jnp.where(low_lane, tail[s : s + 16], tail[s + 16 : s + 32])
        halves.append(jnp.concatenate([main[s : s + 32], tails], axis=0))
    keep_taps[...] = jnp.where(me == 0, halves[0], halves[1])
    high, low = split_high_low(jnp.where(me == 0, halves[1], halves[0]))
    send[ROWS : ROWS + GROWS] = high
    send[ROWS + GROWS :] = low
    grad_rt[...] = grad_r[...].T
    for k, s in enumerate(SUM_ORDER):
        z = my_z ^ s
        e = pack_expand(grad_e[pl.ds(pl.multiple_of(z * EROWS, 8), EROWS), :])
        r = pack_reduce(grad_rt[pl.ds(pl.multiple_of(z * RROWS, RROWS), RROWS), :])
        keep[k * SHARD : (k + 1) * SHARD] = jnp.where(me == 0, e, r)
        send[k * SHARD : (k + 1) * SHARD] = jnp.where(me == 0, r, e).astype(bf16)


def finish_kernel(info, held, other, grad_e, grad_r, grad_k):
    first = info[0, CORE] == 0
    grad_e[...] = unpack_expand(jnp.where(first, held[:SHARD], other[:SHARD])) * FACTOR
    grad_r[...] = unpack_reduce(jnp.where(first, other[:SHARD], held[:SHARD])) * FACTOR
    a, b = held[SHARD:], other[SHARD:]
    halves = []
    for half in (jnp.where(first, a, b), jnp.where(first, b, a)):
        tails = jnp.concatenate([half[32:, :TAIL], half[32:, TAIL:]], axis=0)
        halves.append(jnp.concatenate([half[:32], tails], axis=1))
    whole = jnp.concatenate([halves[0][:24], halves[1]], axis=0) * FACTOR
    for dy in range(KS):
        grad_k[dy] = whole[dy * KS : (dy + 1) * KS]


def spread_kernel(info, padded, cotan, kernel, out, planes, summed, taps):
    fill_taps(kernel, taps, True)
    fill_planes(padded, planes)
    conv_planes(planes, taps, summed)

    def blank(j, carry):
        out[j] = jnp.zeros_like(out[j])
        return carry

    lax.fori_loop(info[0, COUNT], CAP, blank, 0)

    def slot(j, carry):
        out[j] = cotan[j].astype(f32) + tile_of(summed, info[0, PLACE + j]).reshape(S, S, C)
        return carry

    lax.fori_loop(0, info[0, COUNT], slot, 0)


def call(kernel, ins, outs, scratch=(), name=None, us=1):
    smem = pl.BlockSpec(memory_space=pltpu.SMEM)
    vmem = pl.BlockSpec(memory_space=pltpu.VMEM)
    specs = [smem if v.dtype == jnp.int32 else vmem for v in ins]
    return pl.pallas_call(
        kernel,
        out_shape=[jax.ShapeDtypeStruct(shape, dtype) for shape, dtype in outs],
        in_specs=specs,
        out_specs=[vmem for _ in outs],
        scratch_shapes=[pltpu.VMEM(*s) if isinstance(s, tuple) else s for s in scratch],
        compiler_params=pltpu.CompilerParams(vmem_limit_bytes=VMEM_LIMIT),
        cost_estimate=pl.CostEstimate(flops=us * 10**9, bytes_accessed=us * 10**6, transcendentals=0),
        name=name,
    )(*ins)


TAP_PLANES = (2, TAPS, 8, LANES)
PLANES, CELLS = (3, HALF, WIDE, LANES), (3, S, SIDE, LANES)


def block_call(*ins):
    return call(
        block_kernel,
        ins,
        [
            ((CAP, S, S, C), f32),
            ((SIDE, SIDE, C), bf16),
            ((ROWS, LANES), f32),
            ((ROWS + 2 * GROWS, LANES), bf16),
            ((GROWS, LANES), f32),
        ],
        [
            (CELLS, f32),
            ((3, TAPS, 8, LANES), f32),
            ((C, FF), f32),
            ((C, FF), bf16),
            ((FF, C), bf16),
            ((CAP, 2, S * S, FF), f32),
            ((CAP, S * S, FF), bf16),
            ((CAP, S * S, FF), bf16),
            ((C, FF), f32),
            ((C, FF), f32),
            ((FF, C), f32),
        ],
        name="block",
        us=14,
    )


def side_rims(canvas):
    core = lax.axis_index("core")
    west_edge = canvas[:, :3].transpose(1, 0, 2)
    east_edge = canvas[:, -3:].transpose(1, 0, 2)
    inner = swap(jnp.where(core == 0, east_edge, west_edge), "core", 1)
    pairs = [(4 * i + a, 4 * i + 3 - a) for i in range(2) for a in range(4)]
    outer = lax.ppermute(jnp.where(core == 0, west_edge, east_edge), ("x", "core"), pairs)
    return inner, jnp.where(lax.axis_index("x") % 2 != core, outer, jnp.zeros_like(outer))


def widen(canvas, inner, outer):
    core = lax.axis_index("core")
    west = jnp.where(core == 0, outer, inner).transpose(1, 0, 2)
    east = jnp.where(core == 0, inner, outer).transpose(1, 0, 2)
    blank = jnp.zeros((SIDE, WIDE - SIDE - 6, C), canvas.dtype)
    return jnp.concatenate([west, canvas, east, blank], axis=1)


def end_rims(widened):
    upper = lax.axis_index("x") // 2
    north_edge, south_edge = widened[:3], widened[-3:]
    near = swap(jnp.where(upper == 0, south_edge, north_edge), "x", 2)
    pairs = [(4 * y + x, 4 * ((y + 1) % 4) + x - 2) for y in range(4) for x in (2, 3)]
    far = lax.ppermute(
        jnp.where(upper == 0, north_edge, south_edge),
        ("y", "x"),
        pairs + [(b, a) for a, b in pairs],
    )
    inside = jnp.where(upper == 0, lax.axis_index("y") > 0, lax.axis_index("y") < 3)
    return near, jnp.where(inside, far, jnp.zeros_like(far))


def pad_ends(widened, near, far):
    upper = lax.axis_index("x") // 2
    north = jnp.where(upper == 0, far, near)
    south = jnp.where(upper == 0, near, far)
    return jnp.concatenate([north, widened, south], axis=0).astype(f32)


def tie(value, *others):
    return lax.optimization_barrier((value, *others))


def rows_sum(own, a, b, c):
    return (own + a) + (b + c)


def join(value):
    return value[:GROWS].astype(f32) + value[GROWS:].astype(f32)


def per_device(
    tile_data,
    cotangent,
    tile_place,
    tile_count,
    kernel,
    norm_gain,
    expand_weight,
    hidden_bias,
    reduce_weight,
):
    scalars = [lax.axis_index(a) for a in ("core", "rep")] + [tile_count[0, 0]]
    info = jnp.concatenate([jnp.stack(scalars).astype(jnp.int32), tile_place[0, 0]])[None]
    tiles, cotan = tile_data[0], cotangent[0]
    (canvas,) = call(
        place_kernel,
        (info, tiles),
        [((SIDE, SIDE, C), bf16)],
        [pltpu.SemaphoreType.DMA((CAP,))],
        name="place",
    )
    inner, outer = side_rims(canvas)
    shards, inner = tie(expand_weight, inner)
    (packed,) = call(
        pack_kernel, (info, shards, reduce_weight), [((SHARD, LANES), bf16)], name="pack", us=0
    )
    held = jnp.stack([packed, swap(packed, "rep", 7)])
    widened = widen(canvas, inner, outer)
    near, far = end_rims(widened)
    held = jnp.concatenate([held, swap(held, "rep", 2)])
    held_got = swap(held, "rep", 1)
    planes, filtered = call(
        field_kernel,
        (pad_ends(widened, near, far), kernel),
        [(PLANES, f32), (CELLS, f32)],
        [(TAP_PLANES, f32)],
        name="field",
        us=0,
    )
    held_got, filtered = tie(held_got, filtered)
    held = jnp.concatenate([held, held_got])
    other = swap(held, "core", 1)
    result, field, keep, send, taps = block_call(
        info,
        planes,
        filtered,
        tiles,
        cotan,
        norm_gain.reshape(1, C),
        hidden_bias.reshape(1, FF),
        held,
        other,
    )
    pair = 2 * SHARD
    got = swap(send, "core", 1)
    inner, outer = side_rims(field)
    held = keep + got[:ROWS].astype(f32)
    taps = taps + join(got[ROWS:])
    high, low = split_high_low(taps)
    got, inner = tie(got, inner)
    widened = widen(field, inner, outer)
    near, far = end_rims(widened)
    sends = [
        jnp.concatenate([held[k * pair : (k + 1) * pair].astype(bf16), high, low]) for k in (1, 2, 3)
    ]
    got = [swap(part, "rep", s) for part, s in zip(sends, (1, 6, 7))]
    (grad_tiles,) = call(
        spread_kernel,
        (info, pad_ends(widened, near, far), cotan, kernel),
        [((CAP, S, S, C), f32)],
        [(PLANES, f32), (CELLS, f32), (TAP_PLANES, f32)],
        name="spread",
        us=0,
    )
    held = rows_sum(held[:pair], *[g[:pair].astype(f32) for g in got])
    taps = rows_sum(high.astype(f32) + low.astype(f32), *[join(g[pair:]) for g in got])
    high, low = split_high_low(taps)
    part, grad_tiles = tie(jnp.concatenate([held[SHARD:].astype(bf16), high, low]), grad_tiles)
    got = swap(part, "rep", 2)
    held = held[:SHARD] + got[:SHARD].astype(f32)
    taps = (high.astype(f32) + low.astype(f32)) + join(got[SHARD:])
    for axis in ("x", "y"):
        part = jnp.concatenate([held.astype(bf16), *split_high_low(taps)])
        parts = [part] + [swap(part, axis, i) for i in (2, 1, 3)]
        held = rows_sum(*[p[:SHARD].astype(f32) for p in parts])
        taps = rows_sum(*[join(p[SHARD:]) for p in parts])
    held = jnp.concatenate([held, taps])
    grad_expand, grad_reduce, grad_kernel = call(
        finish_kernel,
        (info, held, swap(held, "core", 1)),
        [((EROWS, FF), f32), ((RROWS, C), f32), ((KS, KS, C), f32)],
        name="finish",
    )
    return result[None], grad_tiles[None], grad_expand, grad_reduce, grad_kernel


def solution(mesh):
    fine = Mesh(mesh.devices.reshape(4, 4, 2, 8), ("y", "x", "core", "rep"))
    tiles = P("rep", TILE, None, None, None)
    placed = (
        tiles,
        tiles,
        P("rep", TILE, None),
        P("rep", TILE),
        P(),
        P(),
        P("rep", None),
        P(),
        P("rep", None),
    )
    return jax.shard_map(
        per_device,
        mesh=fine,
        in_specs=placed,
        out_specs=(tiles, tiles, P("rep", None), P("rep", None), P()),
        check_vma=False,
    )
```

```python
import functools

import jax
import jax.numpy as jnp
from jax import lax
from jax.experimental import pallas as pl
from jax.experimental.pallas import tpu as pltpu
from jax.sharding import Mesh, PartitionSpec as P

inv_root_two = 0.7071067811865476
inv_root_two_pi = 0.3989422804014327
bf16 = jnp.bfloat16
f32 = jnp.float32
REP_ORDER = (0, 7, 2, 5, 1, 6, 3, 4)
TILE = ("y", "x", "core")
SIZES = {"y": 4, "x": 4, "core": 2, "rep": 8}
C, FF, S, CAP, KS = 192, 768, 16, 4, 7
SIDE = 2 * S
TAPS = KS * KS
HALF = S + 6
WIDE = SIDE + 8
LANES = 128
TAIL = C - LANES
SHARD = C * FF // SIZES["rep"] // LANES
ROWS = SHARD * SIZES["rep"]
EROWS = C // SIZES["rep"]
RROWS = FF // SIZES["rep"]
GROWS = 48
FACTOR = 1.0 / 512.0
VMEM_LIMIT = 48 * 1024 * 1024


def swap(value, axis, bit):
    return lax.ppermute(value, axis, [(i, i ^ bit) for i in range(SIZES[axis])])


def bit_of(axis, bit):
    return (lax.axis_index(axis) // bit) % 2


def dot(left, right, contract):
    return lax.dot_general(left, right, ((contract[:1], contract[1:]), ((), ())), preferred_element_type=f32)


CORE, AT_REP, COUNT, PLACE = 0, 1, 2, 3


def place_kernel(info, tiles, canvas, sems):
    def tile_copy(j):
        p = info[0, PLACE + j]
        row = pl.multiple_of((p // 2) * S, S)
        col = pl.multiple_of((p % 2) * S, S)
        return row, col, pltpu.make_async_copy(
            tiles.at[j], canvas.at[pl.ds(row, S), pl.ds(col, S), :], sems.at[j]
        )

    for j in range(CAP):
        row, col, copy = tile_copy(j)

        @pl.when(j < info[0, COUNT])
        def _():
            copy.start()

        @pl.when(j >= info[0, COUNT])
        def _():
            canvas[pl.ds(row, S), pl.ds(col, S), :] = jnp.zeros((S, S, C), bf16)

    for j in range(CAP):

        @pl.when(j < info[0, COUNT])
        def _():
            tile_copy(j)[2].wait()


def pack_kernel(info, expand, project, packed):
    e, r = pack_expand(expand[...].astype(f32)), pack_reduce(project[...].astype(f32))
    packed[...] = jnp.where(info[0, CORE] == 0, e, r).astype(bf16)


def fill_taps(kernel, taps, flip):
    for dy in range(KS):
        for dx in range(KS):
            row = kernel[KS - 1 - dy, KS - 1 - dx : KS - dx] if flip else kernel[dy, dx : dx + 1]
            both = jnp.concatenate([row[:, LANES:], row[:, LANES:]], axis=1)
            taps[0, dy * KS + dx] = jnp.broadcast_to(row[:, :LANES], (8, LANES))
            taps[1, dy * KS + dx] = jnp.broadcast_to(both, (8, LANES))


def field_kernel(padded, kernel, planes, filtered, taps):
    fill_taps(kernel, taps, False)
    fill_planes(padded, planes)
    conv_planes(planes, taps, filtered)


def fill_planes(padded, planes):
    planes[0] = padded[:HALF, :, :LANES]
    planes[2] = padded[S:, :, :LANES]
    planes[1] = jnp.concatenate([padded[:HALF, :, LANES:], padded[S:, :, LANES:]], axis=-1)


def conv_planes(planes, taps, out):
    def body(step, carry):
        t = step // 4
        col = pl.multiple_of((step % 4) * 8, 8)
        acc = jnp.zeros((S, 8, LANES), f32)
        for dx in range(KS):
            x = planes[t, :, pl.ds(col + dx, 8), :]
            for dy in range(KS):
                acc = acc + x[dy : dy + S] * taps[t % 2, dy * KS + dx]
        out[t, :, pl.ds(col, 8), :] = acc
        return carry

    lax.fori_loop(0, 12, body, 0)


def correlate_planes(planes, field, acc):
    acc[...] = jnp.zeros_like(acc)

    def body(step, carry):
        t = step // 4
        col = pl.multiple_of((step % 4) * 8, 8)
        g = [field[t, row, pl.ds(col, 8), :] for row in range(S)]
        for dx in range(KS):
            sums = [None] * KS
            for row in range(HALF):
                x = planes[t, row, pl.ds(col + dx, 8), :]
                for dy in range(max(0, row - S + 1), min(KS, row + 1)):
                    term = x * g[row - dy]
                    sums[dy] = term if sums[dy] is None else sums[dy] + term
            for dy in range(KS):
                acc[t, dy * KS + dx] += sums[dy]
        return carry

    lax.fori_loop(0, 12, body, 0)


def tile_of(planes, p):
    lower = p // 2
    col = pl.multiple_of((p % 2) * S, S)
    main = planes[2 * lower, :, pl.ds(col, S), :].reshape(S * S, LANES)
    tail = planes[1, :, pl.ds(col, S), :].reshape(S * S, LANES)
    tail = jnp.where(lower == 1, pltpu.roll(tail, TAIL, 1), tail)
    return jnp.concatenate([main, tail[:, :TAIL]], axis=1)


def pack_expand(rows):
    return jnp.concatenate([rows[:, k * LANES : (k + 1) * LANES] for k in range(FF // LANES)], axis=0)


def pack_reduce(rows):
    half = RROWS // 2
    tails = jnp.concatenate([rows[:half, LANES:], rows[half:, LANES:]], axis=1)
    return jnp.concatenate([rows[:, :LANES], tails], axis=0)


def unpack_expand(value):
    return jnp.concatenate([value[k * EROWS : (k + 1) * EROWS] for k in range(FF // LANES)], axis=1)


def unpack_reduce(value):
    tail = value[RROWS:SHARD]
    tails = jnp.concatenate([tail[:, :TAIL], tail[:, TAIL:]], axis=0)
    return jnp.concatenate([value[:RROWS], tails], axis=1)


def split_high_low(value):
    high = value.astype(bf16)
    return high, (value - high.astype(f32)).astype(bf16)


def block_kernel(
    info, planes, filtered, tiles, cotan, gain, bias, held, other,
    result, field_out, keep, send, keep_taps,
    field, tap_acc, expand_wide, expand, project, hidden, active, grad_hidden,
    grad_e, grad_r, grad_rt,
):
    me, my_z = info[0, CORE], info[0, AT_REP]
    for k, s in enumerate(REP_ORDER):
        z = my_z ^ s
        mine, theirs = held[k].astype(f32), other[k].astype(f32)
        rows = pl.ds(pl.multiple_of(z * EROWS, 8), EROWS)
        expand_wide[rows, :] = unpack_expand(jnp.where(me == 0, mine, theirs))
        rows = pl.ds(pl.multiple_of(z * RROWS, RROWS), RROWS)
        project[rows, :] = unpack_reduce(jnp.where(me == 0, theirs, mine)).astype(bf16)
    expand[...] = expand_wide[...].astype(bf16)
    field[...] = jnp.zeros_like(field)
    field_out[...] = jnp.zeros_like(field_out)
    grad_e[...] = jnp.zeros_like(grad_e)
    grad_r[...] = jnp.zeros_like(grad_r)

    def slot(j):
        live = j < info[0, COUNT]
        p = info[0, PLACE + j]
        lower = p // 2
        row = pl.multiple_of(lower * S, S)
        col = pl.multiple_of((p % 2) * S, S)
        x = tile_of(filtered, p)
        spread = x - jnp.sum(x, axis=1, keepdims=True) * (1.0 / C)
        inverse = lax.rsqrt(jnp.sum(spread * spread, axis=1, keepdims=True) * (1.0 / C) + 1e-6)
        normed = spread * inverse
        scaled = (normed * gain[...]).astype(bf16)
        up = jnp.where(live, cotan[j].reshape(S * S, C), jnp.zeros((S * S, C), bf16))
        hidden[j, 0] = dot(scaled, expand[...], (1, 0))
        hidden[j, 1] = dot(up, project[...], (1, 1))

        def gelu(r, carry):
            rows = pl.ds(pl.multiple_of(r * 16, 16), 16)
            h = hidden[j, 0, rows, :] + bias[...]
            cdf = 0.5 * (1.0 + lax.erf(h * inv_root_two))
            slope = cdf + h * jnp.exp(-0.5 * h * h) * inv_root_two_pi
            active[j, rows, :] = (h * cdf).astype(bf16)
            grad_hidden[j, rows, :] = (hidden[j, 1, rows, :] * slope).astype(bf16)
            return carry

        lax.fori_loop(0, S, gelu, 0, unroll=S)
        a, gh = active[j], grad_hidden[j]
        mixed = dot(a, project[...], (1, 0))
        result[j] = jnp.where(live, tiles[j].astype(f32) + mixed.reshape(S, S, C), jnp.zeros((S, S, C), f32))
        grad_e[...] += dot(scaled, gh, (0, 0))
        grad_r[...] += dot(up, a, (0, 0))
        q = dot(gh, expand[...], (1, 1)) * gain[...]
        mean_q = jnp.sum(q, axis=1, keepdims=True) * (1.0 / C)
        mean_qn = jnp.sum(q * normed, axis=1, keepdims=True) * (1.0 / C)
        g = (inverse * (q - mean_q - normed * mean_qn)).astype(bf16)
        field_out[pl.ds(row, S), pl.ds(col, S), :] = g.reshape(S, S, C)
        g = g.astype(f32)
        field[2 * lower, :, pl.ds(col, S), :] = g[:, :LANES].reshape(S, S, LANES)
        tail = jnp.concatenate([g[:, LANES:], g[:, LANES:]], axis=1).reshape(S, S, LANES)
        old = field[1, :, pl.ds(col, S), :]
        side = lax.broadcasted_iota(jnp.int32, (S, S, LANES), 2) // TAIL
        field[1, :, pl.ds(col, S), :] = jnp.where(side == lower, tail, old)

    for j in range(CAP):
        slot(j)

    correlate_planes(planes, field, tap_acc)
    sums = jnp.sum(tap_acc[...], axis=2)
    main = sums[0] + sums[2]
    tail = sums[1] + pltpu.roll(sums[1], TAIL, 1)
    pad = jnp.zeros((7, LANES), f32)
    main = jnp.concatenate([main, pad], axis=0)
    tail = jnp.concatenate([tail, pad], axis=0)
    low_lane = lax.broadcasted_iota(jnp.int32, (16, LANES), 1) < TAIL
    halves = []
    for h in range(2):
        s = 24 * h
        tails = jnp.where(low_lane, tail[s : s + 16], tail[s + 16 : s + 32])
        halves.append(jnp.concatenate([main[s : s + 32], tails], axis=0))
    keep_taps[...] = jnp.where(me == 0, halves[0], halves[1])
    high, low = split_high_low(jnp.where(me == 0, halves[1], halves[0]))
    send[ROWS : ROWS + GROWS] = high
    send[ROWS + GROWS :] = low
    grad_rt[...] = grad_r[...].T
    for k, s in enumerate(REP_ORDER):
        z = my_z ^ s
        e = pack_expand(grad_e[pl.ds(pl.multiple_of(z * EROWS, 8), EROWS), :])
        r = pack_reduce(grad_rt[pl.ds(pl.multiple_of(z * RROWS, RROWS), RROWS), :])
        keep[k * SHARD : (k + 1) * SHARD] = jnp.where(me == 0, e, r)
        send[k * SHARD : (k + 1) * SHARD] = jnp.where(me == 0, r, e).astype(bf16)


def finish_kernel(info, held, other, grad_e, grad_r, grad_k):
    first = info[0, CORE] == 0
    grad_e[...] = unpack_expand(jnp.where(first, held[:SHARD], other[:SHARD])) * FACTOR
    grad_r[...] = unpack_reduce(jnp.where(first, other[:SHARD], held[:SHARD])) * FACTOR
    a, b = held[SHARD:], other[SHARD:]
    halves = []
    for half in (jnp.where(first, a, b), jnp.where(first, b, a)):
        tails = jnp.concatenate([half[32:, :TAIL], half[32:, TAIL:]], axis=0)
        halves.append(jnp.concatenate([half[:32], tails], axis=1))
    whole = jnp.concatenate([halves[0][:24], halves[1]], axis=0) * FACTOR
    for dy in range(KS):
        grad_k[dy] = whole[dy * KS : (dy + 1) * KS]


def spread_kernel(info, padded, cotan, kernel, out, planes, summed, taps):
    fill_taps(kernel, taps, True)
    fill_planes(padded, planes)
    conv_planes(planes, taps, summed)

    def blank(j, carry):
        out[j] = jnp.zeros_like(out[j])
        return carry

    lax.fori_loop(info[0, COUNT], CAP, blank, 0)

    def slot(j, carry):
        out[j] = cotan[j].astype(f32) + tile_of(summed, info[0, PLACE + j]).reshape(S, S, C)
        return carry

    lax.fori_loop(0, info[0, COUNT], slot, 0)


def call(kernel, ins, outs, scratch=(), name=None, us=1):
    smem = pl.BlockSpec(memory_space=pltpu.SMEM)
    vmem = pl.BlockSpec(memory_space=pltpu.VMEM)
    specs = [smem if v.dtype == jnp.int32 else vmem for v in ins]
    return pl.pallas_call(
        kernel,
        out_shape=[jax.ShapeDtypeStruct(shape, dtype) for shape, dtype in outs],
        in_specs=specs,
        out_specs=[vmem for _ in outs],
        scratch_shapes=[pltpu.VMEM(*s) if isinstance(s, tuple) else s for s in scratch],
        compiler_params=pltpu.CompilerParams(vmem_limit_bytes=VMEM_LIMIT),
        cost_estimate=pl.CostEstimate(flops=us * 10**9, bytes_accessed=us * 10**6, transcendentals=0),
        name=name,
    )(*ins)


TAP_PLANES = (2, TAPS, 8, LANES)
PLANES, CELLS = (3, HALF, WIDE, LANES), (3, S, SIDE, LANES)


def block_call(*ins):
    return call(
        block_kernel,
        ins,
        [
            ((CAP, S, S, C), f32),
            ((SIDE, SIDE, C), bf16),
            ((ROWS, LANES), f32),
            ((ROWS + 2 * GROWS, LANES), bf16),
            ((GROWS, LANES), f32),
        ],
        [
            (CELLS, f32),
            ((3, TAPS, 8, LANES), f32),
            ((C, FF), f32),
            ((C, FF), bf16),
            ((FF, C), bf16),
            ((CAP, 2, S * S, FF), f32),
            ((CAP, S * S, FF), bf16),
            ((CAP, S * S, FF), bf16),
            ((C, FF), f32),
            ((C, FF), f32),
            ((FF, C), f32),
        ],
        name="block",
        us=14,
    )


def side_rims(canvas):
    core = lax.axis_index("core")
    west_edge = canvas[:, :3].transpose(1, 0, 2)
    east_edge = canvas[:, -3:].transpose(1, 0, 2)
    inner = swap(jnp.where(core == 0, east_edge, west_edge), "core", 1)
    pairs = [(4 * i + a, 4 * i + 3 - a) for i in range(2) for a in range(4)]
    outer = lax.ppermute(jnp.where(core == 0, west_edge, east_edge), ("x", "core"), pairs)
    return inner, jnp.where(lax.axis_index("x") % 2 != core, outer, jnp.zeros_like(outer))


def widen(canvas, inner, outer):
    core = lax.axis_index("core")
    west = jnp.where(core == 0, outer, inner).transpose(1, 0, 2)
    east = jnp.where(core == 0, inner, outer).transpose(1, 0, 2)
    blank = jnp.zeros((SIDE, WIDE - SIDE - 6, C), canvas.dtype)
    return jnp.concatenate([west, canvas, east, blank], axis=1)


def end_rims(widened):
    upper = lax.axis_index("x") // 2
    north_edge, south_edge = widened[:3], widened[-3:]
    near = swap(jnp.where(upper == 0, south_edge, north_edge), "x", 2)
    pairs = [(4 * y + x, 4 * ((y + 1) % 4) + x - 2) for y in range(4) for x in (2, 3)]
    far = lax.ppermute(
        jnp.where(upper == 0, north_edge, south_edge),
        ("y", "x"),
        pairs + [(b, a) for a, b in pairs],
    )
    inside = jnp.where(upper == 0, lax.axis_index("y") > 0, lax.axis_index("y") < 3)
    return near, jnp.where(inside, far, jnp.zeros_like(far))


def pad_ends(widened, near, far):
    upper = lax.axis_index("x") // 2
    north = jnp.where(upper == 0, far, near)
    south = jnp.where(upper == 0, near, far)
    return jnp.concatenate([north, widened, south], axis=0).astype(f32)


def tie(value, *others):
    return lax.optimization_barrier((value, *others))


def rows_sum(own, a, b, c):
    return (own + a) + (b + c)


def join(value):
    return value[:GROWS].astype(f32) + value[GROWS:].astype(f32)


def per_device(
    tile_data,
    cotangent,
    tile_place,
    tile_count,
    kernel,
    norm_gain,
    expand_weight,
    hidden_bias,
    reduce_weight,
):
    scalars = [lax.axis_index(a) for a in ("core", "rep")] + [tile_count[0, 0]]
    info = jnp.concatenate([jnp.stack(scalars).astype(jnp.int32), tile_place[0, 0]])[None]
    tiles, cotan = tile_data[0], cotangent[0]
    (canvas,) = call(
        place_kernel,
        (info, tiles),
        [((SIDE, SIDE, C), bf16)],
        [pltpu.SemaphoreType.DMA((CAP,))],
        name="place",
    )
    inner, outer = side_rims(canvas)
    shards, inner = tie(expand_weight, inner)
    (packed,) = call(
        pack_kernel, (info, shards, reduce_weight), [((SHARD, LANES), bf16)], name="pack", us=0
    )
    held = jnp.stack([packed, swap(packed, "rep", 7)])
    widened = widen(canvas, inner, outer)
    near, far = end_rims(widened)
    held = jnp.concatenate([held, swap(held, "rep", 2)])
    held_got = swap(held, "rep", 1)
    planes, filtered = call(
        field_kernel,
        (pad_ends(widened, near, far), kernel),
        [(PLANES, f32), (CELLS, f32)],
        [(TAP_PLANES, f32)],
        name="field",
        us=0,
    )
    held_got, filtered = tie(held_got, filtered)
    held = jnp.concatenate([held, held_got])
    other = swap(held, "core", 1)
    result, field, keep, send, taps = block_call(
        info,
        planes,
        filtered,
        tiles,
        cotan,
        norm_gain.reshape(1, C),
        hidden_bias.reshape(1, FF),
        held,
        other,
    )
    got = swap(send, "core", 1)
    inner, outer = side_rims(field)
    held = keep + got[:ROWS].astype(f32)
    taps = taps + join(got[ROWS:])

    def halve(held, taps, bits, *after):
        half = held.shape[0] // 2
        high, low = split_high_low(taps)
        part = jnp.concatenate([held[half:].astype(bf16), high, low])
        part = tie(part, *after)[0]
        got = swap(part, "rep", bits)
        return (
            held[:half] + got[:half].astype(f32),
            (high.astype(f32) + low.astype(f32)) + join(got[half:]),
        )

    got, inner = tie(got, inner)
    widened = widen(field, inner, outer)
    near, far = end_rims(widened)
    held, taps = halve(held, taps, 1)
    held, near = tie(held, near)
    (grad_tiles,) = call(
        spread_kernel,
        (info, pad_ends(widened, near, far), cotan, kernel),
        [((CAP, S, S, C), f32)],
        [(PLANES, f32), (CELLS, f32), (TAP_PLANES, f32)],
        name="spread",
        us=0,
    )
    held, taps = halve(held, taps, 2)
    held, taps = halve(held, taps, 7, grad_tiles)
    for axis in ("x", "y"):
        part = jnp.concatenate([held.astype(bf16), *split_high_low(taps)])
        parts = [part] + [swap(part, axis, i) for i in (2, 1, 3)]
        held = rows_sum(*[p[:SHARD].astype(f32) for p in parts])
        taps = rows_sum(*[join(p[SHARD:]) for p in parts])
    held = jnp.concatenate([held, taps])
    grad_expand, grad_reduce, grad_kernel = call(
        finish_kernel,
        (info, held, swap(held, "core", 1)),
        [((EROWS, FF), f32), ((RROWS, C), f32), ((KS, KS, C), f32)],
        name="finish",
    )
    return result[None], grad_tiles[None], grad_expand, grad_reduce, grad_kernel


def solution(mesh):
    fine = Mesh(mesh.devices.reshape(4, 4, 2, 8), ("y", "x", "core", "rep"))
    tiles = P("rep", TILE, None, None, None)
    placed = (
        tiles,
        tiles,
        P("rep", TILE, None),
        P("rep", TILE),
        P(),
        P(),
        P("rep", None),
        P(),
        P("rep", None),
    )
    return jax.shard_map(
        per_device,
        mesh=fine,
        in_specs=placed,
        out_specs=(tiles, tiles, P("rep", None), P("rep", None), P()),
        check_vma=False,
    )
```

```python
import functools

import jax
import jax.numpy as jnp
from jax import lax
from jax.experimental import pallas as pl
from jax.experimental.pallas import tpu as pltpu
from jax.sharding import Mesh, PartitionSpec as P

inv_root_two = 0.7071067811865476
inv_root_two_pi = 0.3989422804014327
bf16 = jnp.bfloat16
f32 = jnp.float32
REP_ORDER = (0, 7, 2, 5, 1, 6, 3, 4)
TILE = ("y", "x", "core")
SIZES = {"y": 4, "x": 4, "core": 2, "rep": 8}
C, FF, S, CAP, KS = 192, 768, 16, 4, 7
SIDE = 2 * S
TAPS = KS * KS
HALF = S + 6
WIDE = SIDE + 8
LANES = 128
TAIL = C - LANES
SHARD = C * FF // SIZES["rep"] // LANES
ROWS = SHARD * SIZES["rep"]
EROWS = C // SIZES["rep"]
RROWS = FF // SIZES["rep"]
GROWS = 48
FACTOR = 1.0 / 512.0
VMEM_LIMIT = 48 * 1024 * 1024


def swap(value, axis, bit):
    return lax.ppermute(value, axis, [(i, i ^ bit) for i in range(SIZES[axis])])


def bit_of(axis, bit):
    return (lax.axis_index(axis) // bit) % 2


def dot(left, right, contract):
    return lax.dot_general(left, right, ((contract[:1], contract[1:]), ((), ())), preferred_element_type=f32)


CORE, AT_REP, COUNT, PLACE = 0, 1, 2, 3


def place_kernel(info, tiles, canvas, sems):
    def tile_copy(j):
        p = info[0, PLACE + j]
        row = pl.multiple_of((p // 2) * S, S)
        col = pl.multiple_of((p % 2) * S, S)
        return row, col, pltpu.make_async_copy(
            tiles.at[j], canvas.at[pl.ds(row, S), pl.ds(col, S), :], sems.at[j]
        )

    for j in range(CAP):
        row, col, copy = tile_copy(j)

        @pl.when(j < info[0, COUNT])
        def _():
            copy.start()

        @pl.when(j >= info[0, COUNT])
        def _():
            canvas[pl.ds(row, S), pl.ds(col, S), :] = jnp.zeros((S, S, C), bf16)

    for j in range(CAP):

        @pl.when(j < info[0, COUNT])
        def _():
            tile_copy(j)[2].wait()


def pack_kernel(info, expand, project, packed):
    e, r = pack_expand(expand[...].astype(f32)), pack_reduce(project[...].astype(f32))
    packed[...] = jnp.where(info[0, CORE] == 0, e, r).astype(bf16)


def fill_taps(kernel, taps, flip):
    for dy in range(KS):
        for dx in range(KS):
            row = kernel[KS - 1 - dy, KS - 1 - dx : KS - dx] if flip else kernel[dy, dx : dx + 1]
            both = jnp.concatenate([row[:, LANES:], row[:, LANES:]], axis=1)
            taps[0, dy * KS + dx] = jnp.broadcast_to(row[:, :LANES], (8, LANES))
            taps[1, dy * KS + dx] = jnp.broadcast_to(both, (8, LANES))


def field_kernel(padded, kernel, planes, filtered, taps):
    fill_taps(kernel, taps, False)
    fill_planes(padded, planes)
    conv_planes(planes, taps, filtered)


def fill_planes(padded, planes):
    planes[0] = padded[:HALF, :, :LANES]
    planes[2] = padded[S:, :, :LANES]
    planes[1] = jnp.concatenate([padded[:HALF, :, LANES:], padded[S:, :, LANES:]], axis=-1)


def conv_planes(planes, taps, out, first=0, last=3):
    def body(step, carry):
        t = step // 4
        col = pl.multiple_of((step % 4) * 8, 8)
        acc = jnp.zeros((S, 8, LANES), f32)
        for dx in range(KS):
            x = planes[t, :, pl.ds(col + dx, 8), :]
            for dy in range(KS):
                acc = acc + x[dy : dy + S] * taps[t % 2, dy * KS + dx]
        out[t, :, pl.ds(col, 8), :] = acc
        return carry

    lax.fori_loop(4 * first, 4 * last, body, 0)


def correlate_planes(planes, field, acc):
    acc[...] = jnp.zeros_like(acc)

    def body(step, carry):
        t = step // 4
        col = pl.multiple_of((step % 4) * 8, 8)
        g = [field[t, row, pl.ds(col, 8), :] for row in range(S)]
        for dx in range(KS):
            sums = [None] * KS
            for row in range(HALF):
                x = planes[t, row, pl.ds(col + dx, 8), :]
                for dy in range(max(0, row - S + 1), min(KS, row + 1)):
                    term = x * g[row - dy]
                    sums[dy] = term if sums[dy] is None else sums[dy] + term
            for dy in range(KS):
                acc[t, dy * KS + dx] += sums[dy]
        return carry

    lax.fori_loop(0, 12, body, 0)


def tile_of(planes, p):
    lower = p // 2
    col = pl.multiple_of((p % 2) * S, S)
    main = planes[2 * lower, :, pl.ds(col, S), :].reshape(S * S, LANES)
    tail = planes[1, :, pl.ds(col, S), :].reshape(S * S, LANES)
    tail = jnp.where(lower == 1, pltpu.roll(tail, TAIL, 1), tail)
    return jnp.concatenate([main, tail[:, :TAIL]], axis=1)


def pack_expand(rows):
    return jnp.concatenate([rows[:, k * LANES : (k + 1) * LANES] for k in range(FF // LANES)], axis=0)


def pack_reduce(rows):
    half = RROWS // 2
    tails = jnp.concatenate([rows[:half, LANES:], rows[half:, LANES:]], axis=1)
    return jnp.concatenate([rows[:, :LANES], tails], axis=0)


def unpack_expand(value):
    return jnp.concatenate([value[k * EROWS : (k + 1) * EROWS] for k in range(FF // LANES)], axis=1)


def unpack_reduce(value):
    tail = value[RROWS:SHARD]
    tails = jnp.concatenate([tail[:, :TAIL], tail[:, TAIL:]], axis=0)
    return jnp.concatenate([value[:RROWS], tails], axis=1)


def split_high_low(value):
    high = value.astype(bf16)
    return high, (value - high.astype(f32)).astype(bf16)


def block_kernel(
    info, planes, filtered, tiles, cotan, gain, bias, held, other,
    result, field_out, keep, send, keep_taps,
    field, tap_acc, expand_wide, expand, project, hidden, active, grad_hidden,
    grad_e, grad_r, grad_rt,
):
    me, my_z = info[0, CORE], info[0, AT_REP]
    for k, s in enumerate(REP_ORDER):
        z = my_z ^ s
        mine, theirs = held[k].astype(f32), other[k].astype(f32)
        rows = pl.ds(pl.multiple_of(z * EROWS, 8), EROWS)
        expand_wide[rows, :] = unpack_expand(jnp.where(me == 0, mine, theirs))
        rows = pl.ds(pl.multiple_of(z * RROWS, RROWS), RROWS)
        project[rows, :] = unpack_reduce(jnp.where(me == 0, theirs, mine)).astype(bf16)
    expand[...] = expand_wide[...].astype(bf16)
    field[...] = jnp.zeros_like(field)
    field_out[...] = jnp.zeros_like(field_out)
    grad_e[...] = jnp.zeros_like(grad_e)
    grad_r[...] = jnp.zeros_like(grad_r)

    def slot(j):
        live = j < info[0, COUNT]
        p = info[0, PLACE + j]
        lower = p // 2
        row = pl.multiple_of(lower * S, S)
        col = pl.multiple_of((p % 2) * S, S)
        x = tile_of(filtered, p)
        spread = x - jnp.sum(x, axis=1, keepdims=True) * (1.0 / C)
        inverse = lax.rsqrt(jnp.sum(spread * spread, axis=1, keepdims=True) * (1.0 / C) + 1e-6)
        normed = spread * inverse
        scaled = (normed * gain[...]).astype(bf16)
        up = jnp.where(live, cotan[j].reshape(S * S, C), jnp.zeros((S * S, C), bf16))
        hidden[j, 0] = dot(scaled, expand[...], (1, 0))
        hidden[j, 1] = dot(up, project[...], (1, 1))

        def gelu(r, carry):
            rows = pl.ds(pl.multiple_of(r * 16, 16), 16)
            h = hidden[j, 0, rows, :] + bias[...]
            cdf = 0.5 * (1.0 + lax.erf(h * inv_root_two))
            slope = cdf + h * jnp.exp(-0.5 * h * h) * inv_root_two_pi
            active[j, rows, :] = (h * cdf).astype(bf16)
            grad_hidden[j, rows, :] = (hidden[j, 1, rows, :] * slope).astype(bf16)
            return carry

        lax.fori_loop(0, S, gelu, 0, unroll=S)
        a, gh = active[j], grad_hidden[j]
        mixed = dot(a, project[...], (1, 0))
        result[j] = jnp.where(live, tiles[j].astype(f32) + mixed.reshape(S, S, C), jnp.zeros((S, S, C), f32))
        grad_e[...] += dot(scaled, gh, (0, 0))
        grad_r[...] += dot(up, a, (0, 0))
        q = dot(gh, expand[...], (1, 1)) * gain[...]
        mean_q = jnp.sum(q, axis=1, keepdims=True) * (1.0 / C)
        mean_qn = jnp.sum(q * normed, axis=1, keepdims=True) * (1.0 / C)
        g = (inverse * (q - mean_q - normed * mean_qn)).astype(bf16)
        field_out[pl.ds(row, S), pl.ds(col, S), :] = g.reshape(S, S, C)
        g = g.astype(f32)
        field[2 * lower, :, pl.ds(col, S), :] = g[:, :LANES].reshape(S, S, LANES)
        tail = jnp.concatenate([g[:, LANES:], g[:, LANES:]], axis=1).reshape(S, S, LANES)
        old = field[1, :, pl.ds(col, S), :]
        side = lax.broadcasted_iota(jnp.int32, (S, S, LANES), 2) // TAIL
        field[1, :, pl.ds(col, S), :] = jnp.where(side == lower, tail, old)

    for j in range(CAP):
        slot(j)

    correlate_planes(planes, field, tap_acc)
    sums = jnp.sum(tap_acc[...], axis=2)
    main = sums[0] + sums[2]
    tail = sums[1] + pltpu.roll(sums[1], TAIL, 1)
    pad = jnp.zeros((7, LANES), f32)
    main = jnp.concatenate([main, pad], axis=0)
    tail = jnp.concatenate([tail, pad], axis=0)
    low_lane = lax.broadcasted_iota(jnp.int32, (16, LANES), 1) < TAIL
    halves = []
    for h in range(2):
        s = 24 * h
        tails = jnp.where(low_lane, tail[s : s + 16], tail[s + 16 : s + 32])
        halves.append(jnp.concatenate([main[s : s + 32], tails], axis=0))
    keep_taps[...] = jnp.where(me == 0, halves[0], halves[1])
    high, low = split_high_low(jnp.where(me == 0, halves[1], halves[0]))
    send[ROWS : ROWS + GROWS] = high
    send[ROWS + GROWS :] = low
    grad_rt[...] = grad_r[...].T
    for k, s in enumerate(REP_ORDER):
        z = my_z ^ s
        e = pack_expand(grad_e[pl.ds(pl.multiple_of(z * EROWS, 8), EROWS), :])
        r = pack_reduce(grad_rt[pl.ds(pl.multiple_of(z * RROWS, RROWS), RROWS), :])
        keep[k * SHARD : (k + 1) * SHARD] = jnp.where(me == 0, e, r)
        send[k * SHARD : (k + 1) * SHARD] = jnp.where(me == 0, r, e).astype(bf16)


def finish_kernel(info, held, other, grad_e, grad_r, grad_k):
    first = info[0, CORE] == 0
    grad_e[...] = unpack_expand(jnp.where(first, held[:SHARD], other[:SHARD])) * FACTOR
    grad_r[...] = unpack_reduce(jnp.where(first, other[:SHARD], held[:SHARD])) * FACTOR
    a, b = held[SHARD:], other[SHARD:]
    halves = []
    for half in (jnp.where(first, a, b), jnp.where(first, b, a)):
        tails = jnp.concatenate([half[32:, :TAIL], half[32:, TAIL:]], axis=0)
        halves.append(jnp.concatenate([half[:32], tails], axis=1))
    whole = jnp.concatenate([halves[0][:24], halves[1]], axis=0) * FACTOR
    for dy in range(KS):
        grad_k[dy] = whole[dy * KS : (dy + 1) * KS]


def spread_kernel(padded, kernel, planes, summed, taps):
    fill_taps(kernel, taps, True)
    fill_planes(padded, planes)
    conv_planes(planes, taps, summed, 0, 2)


def emit_kernel(info, planes, partial, cotan, kernel, out, summed, taps):
    fill_taps(kernel, taps, True)
    summed[:2] = partial[:2]
    conv_planes(planes, taps, summed, 2, 3)

    def blank(j, carry):
        out[j] = jnp.zeros_like(out[j])
        return carry

    lax.fori_loop(info[0, COUNT], CAP, blank, 0)

    def slot(j, carry):
        out[j] = cotan[j].astype(f32) + tile_of(summed, info[0, PLACE + j]).reshape(S, S, C)
        return carry

    lax.fori_loop(0, info[0, COUNT], slot, 0)


def call(kernel, ins, outs, scratch=(), name=None, us=1):
    smem = pl.BlockSpec(memory_space=pltpu.SMEM)
    vmem = pl.BlockSpec(memory_space=pltpu.VMEM)
    specs = [smem if v.dtype == jnp.int32 else vmem for v in ins]
    return pl.pallas_call(
        kernel,
        out_shape=[jax.ShapeDtypeStruct(shape, dtype) for shape, dtype in outs],
        in_specs=specs,
        out_specs=[vmem for _ in outs],
        scratch_shapes=[pltpu.VMEM(*s) if isinstance(s, tuple) else s for s in scratch],
        compiler_params=pltpu.CompilerParams(vmem_limit_bytes=VMEM_LIMIT),
        cost_estimate=pl.CostEstimate(flops=us * 10**9, bytes_accessed=us * 10**6, transcendentals=0),
        name=name,
    )(*ins)


TAP_PLANES = (2, TAPS, 8, LANES)
PLANES, CELLS = (3, HALF, WIDE, LANES), (3, S, SIDE, LANES)


def block_call(*ins):
    return call(
        block_kernel,
        ins,
        [
            ((CAP, S, S, C), f32),
            ((SIDE, SIDE, C), bf16),
            ((ROWS, LANES), f32),
            ((ROWS + 2 * GROWS, LANES), bf16),
            ((GROWS, LANES), f32),
        ],
        [
            (CELLS, f32),
            ((3, TAPS, 8, LANES), f32),
            ((C, FF), f32),
            ((C, FF), bf16),
            ((FF, C), bf16),
            ((CAP, 2, S * S, FF), f32),
            ((CAP, S * S, FF), bf16),
            ((CAP, S * S, FF), bf16),
            ((C, FF), f32),
            ((C, FF), f32),
            ((FF, C), f32),
        ],
        name="block",
        us=14,
    )


def side_rims(canvas):
    core = lax.axis_index("core")
    west_edge = canvas[:, :3].transpose(1, 0, 2)
    east_edge = canvas[:, -3:].transpose(1, 0, 2)
    inner = swap(jnp.where(core == 0, east_edge, west_edge), "core", 1)
    pairs = [(4 * i + a, 4 * i + 3 - a) for i in range(2) for a in range(4)]
    outer = lax.ppermute(jnp.where(core == 0, west_edge, east_edge), ("x", "core"), pairs)
    return inner, jnp.where(lax.axis_index("x") % 2 != core, outer, jnp.zeros_like(outer))


def widen(canvas, inner, outer):
    core = lax.axis_index("core")
    west = jnp.where(core == 0, outer, inner).transpose(1, 0, 2)
    east = jnp.where(core == 0, inner, outer).transpose(1, 0, 2)
    blank = jnp.zeros((SIDE, WIDE - SIDE - 6, C), canvas.dtype)
    return jnp.concatenate([west, canvas, east, blank], axis=1)


def end_rims(widened):
    upper = lax.axis_index("x") // 2
    north_edge, south_edge = widened[:3], widened[-3:]
    near = swap(jnp.where(upper == 0, south_edge, north_edge), "x", 2)
    pairs = [(4 * y + x, 4 * ((y + 1) % 4) + x - 2) for y in range(4) for x in (2, 3)]
    far = lax.ppermute(
        jnp.where(upper == 0, north_edge, south_edge),
        ("y", "x"),
        pairs + [(b, a) for a, b in pairs],
    )
    inside = jnp.where(upper == 0, lax.axis_index("y") > 0, lax.axis_index("y") < 3)
    return near, jnp.where(inside, far, jnp.zeros_like(far))


def pad_ends(widened, near, far):
    upper = lax.axis_index("x") // 2
    north = jnp.where(upper == 0, far, near)
    south = jnp.where(upper == 0, near, far)
    return jnp.concatenate([north, widened, south], axis=0).astype(f32)


def tie(value, *others):
    return lax.optimization_barrier((value, *others))


def rows_sum(own, a, b, c):
    return (own + a) + (b + c)


def join(value):
    return value[:GROWS].astype(f32) + value[GROWS:].astype(f32)


def per_device(
    tile_data,
    cotangent,
    tile_place,
    tile_count,
    kernel,
    norm_gain,
    expand_weight,
    hidden_bias,
    reduce_weight,
):
    scalars = [lax.axis_index(a) for a in ("core", "rep")] + [tile_count[0, 0]]
    info = jnp.concatenate([jnp.stack(scalars).astype(jnp.int32), tile_place[0, 0]])[None]
    tiles, cotan = tile_data[0], cotangent[0]
    (canvas,) = call(
        place_kernel,
        (info, tiles),
        [((SIDE, SIDE, C), bf16)],
        [pltpu.SemaphoreType.DMA((CAP,))],
        name="place",
    )
    inner, outer = side_rims(canvas)
    shards, inner = tie(expand_weight, inner)
    (packed,) = call(
        pack_kernel, (info, shards, reduce_weight), [((SHARD, LANES), bf16)], name="pack", us=0
    )
    held = jnp.stack([packed, swap(packed, "rep", 7)])
    widened = widen(canvas, inner, outer)
    near, far = end_rims(widened)
    held = jnp.concatenate([held, swap(held, "rep", 2)])
    held_got = swap(held, "rep", 1)
    planes, filtered = call(
        field_kernel,
        (pad_ends(widened, near, far), kernel),
        [(PLANES, f32), (CELLS, f32)],
        [(TAP_PLANES, f32)],
        name="field",
        us=0,
    )
    held_got, filtered = tie(held_got, filtered)
    held = jnp.concatenate([held, held_got])
    other = swap(held, "core", 1)
    result, field, keep, send, taps = block_call(
        info,
        planes,
        filtered,
        tiles,
        cotan,
        norm_gain.reshape(1, C),
        hidden_bias.reshape(1, FF),
        held,
        other,
    )
    got = swap(send, "core", 1)
    inner, outer = side_rims(field)
    held = keep + got[:ROWS].astype(f32)
    taps = taps + join(got[ROWS:])

    def halve(held, taps, bits, *after):
        half = held.shape[0] // 2
        high, low = split_high_low(taps)
        part = jnp.concatenate([held[half:].astype(bf16), high, low])
        part = tie(part, *after)[0]
        got = swap(part, "rep", bits)
        return (
            held[:half] + got[:half].astype(f32),
            (high.astype(f32) + low.astype(f32)) + join(got[half:]),
        )

    got, inner = tie(got, inner)
    widened = widen(field, inner, outer)
    near, far = end_rims(widened)
    held, taps = halve(held, taps, 1)
    near = tie(near, held)[0]
    planes, summed = call(
        spread_kernel,
        (pad_ends(widened, near, far), kernel),
        [(PLANES, f32), (CELLS, f32)],
        [(TAP_PLANES, f32)],
        name="spread",
        us=0,
    )
    held, taps = halve(held, taps, 2)
    held, taps = halve(held, taps, 7, summed)
    (grad_tiles,) = call(
        emit_kernel,
        (info, planes, summed, cotan, kernel),
        [((CAP, S, S, C), f32)],
        [(CELLS, f32), (TAP_PLANES, f32)],
        name="emit",
        us=0,
    )
    taps, grad_tiles = tie(taps, grad_tiles)
    for axis in ("x", "y"):
        part = jnp.concatenate([held.astype(bf16), *split_high_low(taps)])
        parts = [part] + [swap(part, axis, i) for i in (2, 1, 3)]
        held = rows_sum(*[p[:SHARD].astype(f32) for p in parts])
        taps = rows_sum(*[join(p[SHARD:]) for p in parts])
    held = jnp.concatenate([held, taps])
    grad_expand, grad_reduce, grad_kernel = call(
        finish_kernel,
        (info, held, swap(held, "core", 1)),
        [((EROWS, FF), f32), ((RROWS, C), f32), ((KS, KS, C), f32)],
        name="finish",
    )
    return result[None], grad_tiles[None], grad_expand, grad_reduce, grad_kernel


def solution(mesh):
    fine = Mesh(mesh.devices.reshape(4, 4, 2, 8), ("y", "x", "core", "rep"))
    tiles = P("rep", TILE, None, None, None)
    placed = (
        tiles,
        tiles,
        P("rep", TILE, None),
        P("rep", TILE),
        P(),
        P(),
        P("rep", None),
        P(),
        P("rep", None),
    )
    return jax.shard_map(
        per_device,
        mesh=fine,
        in_specs=placed,
        out_specs=(tiles, tiles, P("rep", None), P("rep", None), P()),
        check_vma=False,
    )
```

```python
import functools

import jax
import jax.numpy as jnp
from jax import lax
from jax.experimental import pallas as pl
from jax.experimental.pallas import tpu as pltpu
from jax.sharding import Mesh, PartitionSpec as P

inv_root_two = 0.7071067811865476
inv_root_two_pi = 0.3989422804014327
bf16 = jnp.bfloat16
f32 = jnp.float32
REP_ORDER = (0, 7, 2, 5, 1, 6, 3, 4)
TILE = ("y", "x", "core")
SIZES = {"y": 4, "x": 4, "core": 2, "rep": 8}
C, FF, S, CAP, KS = 192, 768, 16, 4, 7
SIDE = 2 * S
TAPS = KS * KS
HALF = S + 6
WIDE = SIDE + 8
LANES = 128
TAIL = C - LANES
SHARD = C * FF // SIZES["rep"] // LANES
ROWS = SHARD * SIZES["rep"]
EROWS = C // SIZES["rep"]
RROWS = FF // SIZES["rep"]
GROWS = 48
FACTOR = 1.0 / 512.0
VMEM_LIMIT = 48 * 1024 * 1024


def swap(value, axis, bit):
    return lax.ppermute(value, axis, [(i, i ^ bit) for i in range(SIZES[axis])])


def bit_of(axis, bit):
    return (lax.axis_index(axis) // bit) % 2


def dot(left, right, contract):
    return lax.dot_general(left, right, ((contract[:1], contract[1:]), ((), ())), preferred_element_type=f32)


CORE, AT_REP, COUNT, PLACE = 0, 1, 2, 3


def place_kernel(info, tiles, canvas, sems):
    def tile_copy(j):
        p = info[0, PLACE + j]
        row = pl.multiple_of((p // 2) * S, S)
        col = pl.multiple_of((p % 2) * S, S)
        return row, col, pltpu.make_async_copy(
            tiles.at[j], canvas.at[pl.ds(row, S), pl.ds(col, S), :], sems.at[j]
        )

    for j in range(CAP):
        row, col, copy = tile_copy(j)

        @pl.when(j < info[0, COUNT])
        def _():
            copy.start()

        @pl.when(j >= info[0, COUNT])
        def _():
            canvas[pl.ds(row, S), pl.ds(col, S), :] = jnp.zeros((S, S, C), bf16)

    for j in range(CAP):

        @pl.when(j < info[0, COUNT])
        def _():
            tile_copy(j)[2].wait()


def pack_kernel(info, expand, project, packed):
    e, r = pack_expand(expand[...].astype(f32)), pack_reduce(project[...].astype(f32))
    packed[...] = jnp.where(info[0, CORE] == 0, e, r).astype(bf16)


def fill_taps(kernel, taps, flip):
    for dy in range(KS):
        for dx in range(KS):
            row = kernel[KS - 1 - dy, KS - 1 - dx : KS - dx] if flip else kernel[dy, dx : dx + 1]
            both = jnp.concatenate([row[:, LANES:], row[:, LANES:]], axis=1)
            taps[0, dy * KS + dx] = jnp.broadcast_to(row[:, :LANES], (8, LANES))
            taps[1, dy * KS + dx] = jnp.broadcast_to(both, (8, LANES))


def field_kernel(padded, kernel, planes, filtered, taps):
    fill_taps(kernel, taps, False)
    fill_planes(padded, planes)
    conv_planes(planes, taps, filtered)


def fill_planes(padded, planes):
    planes[0] = padded[:HALF, :, :LANES]
    planes[2] = padded[S:, :, :LANES]
    planes[1] = jnp.concatenate([padded[:HALF, :, LANES:], padded[S:, :, LANES:]], axis=-1)


def conv_planes(planes, taps, out, first=0, last=3):
    def body(step, carry):
        t = step // 4
        col = pl.multiple_of((step % 4) * 8, 8)
        acc = jnp.zeros((S, 8, LANES), f32)
        for dx in range(KS):
            x = planes[t, :, pl.ds(col + dx, 8), :]
            for dy in range(KS):
                acc = acc + x[dy : dy + S] * taps[t % 2, dy * KS + dx]
        out[t, :, pl.ds(col, 8), :] = acc
        return carry

    lax.fori_loop(4 * first, 4 * last, body, 0)


def correlate_planes(planes, field, acc):
    acc[...] = jnp.zeros_like(acc)

    def body(step, carry):
        t = step // 4
        col = pl.multiple_of((step % 4) * 8, 8)
        g = [field[t, row, pl.ds(col, 8), :] for row in range(S)]
        for dx in range(KS):
            sums = [None] * KS
            for row in range(HALF):
                x = planes[t, row, pl.ds(col + dx, 8), :]
                for dy in range(max(0, row - S + 1), min(KS, row + 1)):
                    term = x * g[row - dy]
                    sums[dy] = term if sums[dy] is None else sums[dy] + term
            for dy in range(KS):
                acc[t, dy * KS + dx] += sums[dy]
        return carry

    lax.fori_loop(0, 12, body, 0)


def tile_of(planes, p):
    lower = p // 2
    col = pl.multiple_of((p % 2) * S, S)
    main = planes[2 * lower, :, pl.ds(col, S), :].reshape(S * S, LANES)
    tail = planes[1, :, pl.ds(col, S), :].reshape(S * S, LANES)
    tail = jnp.where(lower == 1, pltpu.roll(tail, TAIL, 1), tail)
    return jnp.concatenate([main, tail[:, :TAIL]], axis=1)


def pack_expand(rows):
    return jnp.concatenate([rows[:, k * LANES : (k + 1) * LANES] for k in range(FF // LANES)], axis=0)


def pack_reduce(rows):
    half = RROWS // 2
    tails = jnp.concatenate([rows[:half, LANES:], rows[half:, LANES:]], axis=1)
    return jnp.concatenate([rows[:, :LANES], tails], axis=0)


def unpack_expand(value):
    return jnp.concatenate([value[k * EROWS : (k + 1) * EROWS] for k in range(FF // LANES)], axis=1)


def unpack_reduce(value):
    tail = value[RROWS:SHARD]
    tails = jnp.concatenate([tail[:, :TAIL], tail[:, TAIL:]], axis=0)
    return jnp.concatenate([value[:RROWS], tails], axis=1)


def split_high_low(value):
    high = value.astype(bf16)
    return high, (value - high.astype(f32)).astype(bf16)


def block_kernel(
    info, planes, filtered, tiles, cotan, gain, bias, held, other,
    result, field_out, keep, send, keep_taps,
    field, tap_acc, expand_wide, expand, project, hidden, active, grad_hidden,
    grad_e, grad_r, grad_rt,
):
    me, my_z = info[0, CORE], info[0, AT_REP]
    for k, s in enumerate(REP_ORDER):
        z = my_z ^ s
        mine, theirs = held[k].astype(f32), other[k].astype(f32)
        rows = pl.ds(pl.multiple_of(z * EROWS, 8), EROWS)
        expand_wide[rows, :] = unpack_expand(jnp.where(me == 0, mine, theirs))
        rows = pl.ds(pl.multiple_of(z * RROWS, RROWS), RROWS)
        project[rows, :] = unpack_reduce(jnp.where(me == 0, theirs, mine)).astype(bf16)
    expand[...] = expand_wide[...].astype(bf16)
    field[...] = jnp.zeros_like(field)
    field_out[...] = jnp.zeros_like(field_out)
    grad_e[...] = jnp.zeros_like(grad_e)
    grad_r[...] = jnp.zeros_like(grad_r)

    def slot(j):
        live = j < info[0, COUNT]
        p = info[0, PLACE + j]
        lower = p // 2
        row = pl.multiple_of(lower * S, S)
        col = pl.multiple_of((p % 2) * S, S)
        x = tile_of(filtered, p)
        spread = x - jnp.sum(x, axis=1, keepdims=True) * (1.0 / C)
        inverse = lax.rsqrt(jnp.sum(spread * spread, axis=1, keepdims=True) * (1.0 / C) + 1e-6)
        normed = spread * inverse
        scaled = (normed * gain[...]).astype(bf16)
        up = jnp.where(live, cotan[j].reshape(S * S, C), jnp.zeros((S * S, C), bf16))
        hidden[j, 0] = dot(scaled, expand[...], (1, 0))
        hidden[j, 1] = dot(up, project[...], (1, 1))

        def gelu(r, carry):
            rows = pl.ds(pl.multiple_of(r * 16, 16), 16)
            h = hidden[j, 0, rows, :] + bias[...]
            cdf = 0.5 * (1.0 + lax.erf(h * inv_root_two))
            slope = cdf + h * jnp.exp(-0.5 * h * h) * inv_root_two_pi
            active[j, rows, :] = (h * cdf).astype(bf16)
            grad_hidden[j, rows, :] = (hidden[j, 1, rows, :] * slope).astype(bf16)
            return carry

        lax.fori_loop(0, S, gelu, 0, unroll=S)
        a, gh = active[j], grad_hidden[j]
        mixed = dot(a, project[...], (1, 0))
        result[j] = jnp.where(live, tiles[j].astype(f32) + mixed.reshape(S, S, C), jnp.zeros((S, S, C), f32))
        grad_e[...] += dot(scaled, gh, (0, 0))
        grad_r[...] += dot(up, a, (0, 0))
        q = dot(gh, expand[...], (1, 1)) * gain[...]
        mean_q = jnp.sum(q, axis=1, keepdims=True) * (1.0 / C)
        mean_qn = jnp.sum(q * normed, axis=1, keepdims=True) * (1.0 / C)
        g = (inverse * (q - mean_q - normed * mean_qn)).astype(bf16)
        field_out[pl.ds(row, S), pl.ds(col, S), :] = g.reshape(S, S, C)
        g = g.astype(f32)
        field[2 * lower, :, pl.ds(col, S), :] = g[:, :LANES].reshape(S, S, LANES)
        tail = jnp.concatenate([g[:, LANES:], g[:, LANES:]], axis=1).reshape(S, S, LANES)
        old = field[1, :, pl.ds(col, S), :]
        side = lax.broadcasted_iota(jnp.int32, (S, S, LANES), 2) // TAIL
        field[1, :, pl.ds(col, S), :] = jnp.where(side == lower, tail, old)

    for j in range(CAP):
        slot(j)

    correlate_planes(planes, field, tap_acc)
    sums = jnp.sum(tap_acc[...], axis=2)
    main = sums[0] + sums[2]
    tail = sums[1] + pltpu.roll(sums[1], TAIL, 1)
    pad = jnp.zeros((7, LANES), f32)
    main = jnp.concatenate([main, pad], axis=0)
    tail = jnp.concatenate([tail, pad], axis=0)
    low_lane = lax.broadcasted_iota(jnp.int32, (16, LANES), 1) < TAIL
    halves = []
    for h in range(2):
        s = 24 * h
        tails = jnp.where(low_lane, tail[s : s + 16], tail[s + 16 : s + 32])
        halves.append(jnp.concatenate([main[s : s + 32], tails], axis=0))
    keep_taps[...] = jnp.where(me == 0, halves[0], halves[1])
    high, low = split_high_low(jnp.where(me == 0, halves[1], halves[0]))
    send[ROWS : ROWS + GROWS] = high
    send[ROWS + GROWS :] = low
    grad_rt[...] = grad_r[...].T
    for k, s in enumerate(REP_ORDER):
        z = my_z ^ s
        e = pack_expand(grad_e[pl.ds(pl.multiple_of(z * EROWS, 8), EROWS), :])
        r = pack_reduce(grad_rt[pl.ds(pl.multiple_of(z * RROWS, RROWS), RROWS), :])
        keep[k * SHARD : (k + 1) * SHARD] = jnp.where(me == 0, e, r)
        send[k * SHARD : (k + 1) * SHARD] = jnp.where(me == 0, r, e).astype(bf16)


def finish_kernel(info, held, other, grad_e, grad_r, grad_k):
    first = info[0, CORE] == 0
    grad_e[...] = unpack_expand(jnp.where(first, held[:SHARD], other[:SHARD])) * FACTOR
    grad_r[...] = unpack_reduce(jnp.where(first, other[:SHARD], held[:SHARD])) * FACTOR
    a, b = held[SHARD:], other[SHARD:]
    halves = []
    for half in (jnp.where(first, a, b), jnp.where(first, b, a)):
        tails = jnp.concatenate([half[32:, :TAIL], half[32:, TAIL:]], axis=0)
        halves.append(jnp.concatenate([half[:32], tails], axis=1))
    whole = jnp.concatenate([halves[0][:24], halves[1]], axis=0) * FACTOR
    for dy in range(KS):
        grad_k[dy] = whole[dy * KS : (dy + 1) * KS]


def spread_kernel(padded, kernel, planes, summed, taps):
    fill_taps(kernel, taps, True)
    fill_planes(padded, planes)
    conv_planes(planes, taps, summed, 0, 2)


def emit_kernel(info, planes, partial, cotan, kernel, out, summed, taps):
    fill_taps(kernel, taps, True)
    summed[:2] = partial[:2]
    conv_planes(planes, taps, summed, 2, 3)

    def blank(j, carry):
        out[j] = jnp.zeros_like(out[j])
        return carry

    lax.fori_loop(info[0, COUNT], CAP, blank, 0)

    def slot(j, carry):
        out[j] = cotan[j].astype(f32) + tile_of(summed, info[0, PLACE + j]).reshape(S, S, C)
        return carry

    lax.fori_loop(0, info[0, COUNT], slot, 0)


def call(kernel, ins, outs, scratch=(), name=None, us=1):
    smem = pl.BlockSpec(memory_space=pltpu.SMEM)
    vmem = pl.BlockSpec(memory_space=pltpu.VMEM)
    specs = [smem if v.dtype == jnp.int32 else vmem for v in ins]
    return pl.pallas_call(
        kernel,
        out_shape=[jax.ShapeDtypeStruct(shape, dtype) for shape, dtype in outs],
        in_specs=specs,
        out_specs=[vmem for _ in outs],
        scratch_shapes=[pltpu.VMEM(*s) if isinstance(s, tuple) else s for s in scratch],
        compiler_params=pltpu.CompilerParams(vmem_limit_bytes=VMEM_LIMIT),
        cost_estimate=pl.CostEstimate(flops=us * 10**9, bytes_accessed=us * 10**6, transcendentals=0),
        name=name,
    )(*ins)


TAP_PLANES = (2, TAPS, 8, LANES)
PLANES, CELLS = (3, HALF, WIDE, LANES), (3, S, SIDE, LANES)


def block_call(*ins):
    return call(
        block_kernel,
        ins,
        [
            ((CAP, S, S, C), f32),
            ((SIDE, SIDE, C), bf16),
            ((ROWS, LANES), f32),
            ((ROWS + 2 * GROWS, LANES), bf16),
            ((GROWS, LANES), f32),
        ],
        [
            (CELLS, f32),
            ((3, TAPS, 8, LANES), f32),
            ((C, FF), f32),
            ((C, FF), bf16),
            ((FF, C), bf16),
            ((CAP, 2, S * S, FF), f32),
            ((CAP, S * S, FF), bf16),
            ((CAP, S * S, FF), bf16),
            ((C, FF), f32),
            ((C, FF), f32),
            ((FF, C), f32),
        ],
        name="block",
        us=14,
    )


def side_rims(canvas):
    core = lax.axis_index("core")
    west_edge = canvas[:, :3].transpose(1, 0, 2)
    east_edge = canvas[:, -3:].transpose(1, 0, 2)
    inner = swap(jnp.where(core == 0, east_edge, west_edge), "core", 1)
    pairs = [(4 * i + a, 4 * i + 3 - a) for i in range(2) for a in range(4)]
    outer = lax.ppermute(jnp.where(core == 0, west_edge, east_edge), ("x", "core"), pairs)
    return inner, jnp.where(lax.axis_index("x") % 2 != core, outer, jnp.zeros_like(outer))


def widen(canvas, inner, outer):
    core = lax.axis_index("core")
    west = jnp.where(core == 0, outer, inner).transpose(1, 0, 2)
    east = jnp.where(core == 0, inner, outer).transpose(1, 0, 2)
    blank = jnp.zeros((SIDE, WIDE - SIDE - 6, C), canvas.dtype)
    return jnp.concatenate([west, canvas, east, blank], axis=1)


def end_rims(widened):
    upper = lax.axis_index("x") // 2
    north_edge, south_edge = widened[:3], widened[-3:]
    near = swap(jnp.where(upper == 0, south_edge, north_edge), "x", 2)
    pairs = [(4 * y + x, 4 * ((y + 1) % 4) + x - 2) for y in range(4) for x in (2, 3)]
    far = lax.ppermute(
        jnp.where(upper == 0, north_edge, south_edge),
        ("y", "x"),
        pairs + [(b, a) for a, b in pairs],
    )
    inside = jnp.where(upper == 0, lax.axis_index("y") > 0, lax.axis_index("y") < 3)
    return near, jnp.where(inside, far, jnp.zeros_like(far))


def pad_ends(widened, near, far):
    upper = lax.axis_index("x") // 2
    north = jnp.where(upper == 0, far, near)
    south = jnp.where(upper == 0, near, far)
    return jnp.concatenate([north, widened, south], axis=0).astype(f32)


def tie(value, *others):
    return lax.optimization_barrier((value, *others))


def rows_sum(own, a, b, c):
    return (own + a) + (b + c)


def join(value):
    return value[:GROWS].astype(f32) + value[GROWS:].astype(f32)


def per_device(
    tile_data,
    cotangent,
    tile_place,
    tile_count,
    kernel,
    norm_gain,
    expand_weight,
    hidden_bias,
    reduce_weight,
):
    scalars = [lax.axis_index(a) for a in ("core", "rep")] + [tile_count[0, 0]]
    info = jnp.concatenate([jnp.stack(scalars).astype(jnp.int32), tile_place[0, 0]])[None]
    tiles, cotan = tile_data[0], cotangent[0]
    (canvas,) = call(
        place_kernel,
        (info, tiles),
        [((SIDE, SIDE, C), bf16)],
        [pltpu.SemaphoreType.DMA((CAP,))],
        name="place",
    )
    inner, outer = side_rims(canvas)
    shards, inner = tie(expand_weight, inner)
    (packed,) = call(
        pack_kernel, (info, shards, reduce_weight), [((SHARD, LANES), bf16)], name="pack", us=0
    )
    held = jnp.stack([packed, swap(packed, "rep", 7)])
    widened = widen(canvas, inner, outer)
    near, far = end_rims(widened)
    held = jnp.concatenate([held, swap(held, "rep", 2)])
    held_got = swap(held, "rep", 1)
    planes, filtered = call(
        field_kernel,
        (pad_ends(widened, near, far), kernel),
        [(PLANES, f32), (CELLS, f32)],
        [(TAP_PLANES, f32)],
        name="field",
        us=0,
    )
    held_got, filtered = tie(held_got, filtered)
    held = jnp.concatenate([held, held_got])
    other = swap(held, "core", 1)
    result, field, keep, send, taps = block_call(
        info,
        planes,
        filtered,
        tiles,
        cotan,
        norm_gain.reshape(1, C),
        hidden_bias.reshape(1, FF),
        held,
        other,
    )
    got = swap(send, "core", 1)
    inner, outer = side_rims(field)
    held = keep + got[:ROWS].astype(f32)
    taps = taps + join(got[ROWS:])

    def halve(held, taps, bits, *after):
        half = held.shape[0] // 2
        high, low = split_high_low(taps)
        part = jnp.concatenate([held[half:].astype(bf16), high, low])
        part = tie(part, *after)[0]
        got = swap(part, "rep", bits)
        return (
            held[:half] + got[:half].astype(f32),
            (high.astype(f32) + low.astype(f32)) + join(got[half:]),
        )

    got, inner = tie(got, inner)
    widened = widen(field, inner, outer)
    near, far = end_rims(widened)
    held, taps = halve(held, taps, 1)
    near = tie(near, held)[0]
    planes, summed = call(
        spread_kernel,
        (pad_ends(widened, near, far), kernel),
        [(PLANES, f32), (CELLS, f32)],
        [(TAP_PLANES, f32)],
        name="spread",
        us=0,
    )
    held, taps = halve(held, taps, 2)
    held, taps = halve(held, taps, 7, summed)
    (grad_tiles,) = call(
        emit_kernel,
        (info, planes, summed, cotan, kernel),
        [((CAP, S, S, C), f32)],
        [(CELLS, f32), (TAP_PLANES, f32)],
        name="emit",
        us=0,
    )
    taps, grad_tiles = tie(taps, grad_tiles)
    for axis in ("x", "y"):
        part = jnp.concatenate([held.astype(bf16), *split_high_low(taps)])
        parts = [part] + [swap(part, axis, i) for i in (1, 3, 2)]
        held = rows_sum(*[p[:SHARD].astype(f32) for p in parts])
        taps = rows_sum(*[join(p[SHARD:]) for p in parts])
    held = jnp.concatenate([held, taps])
    grad_expand, grad_reduce, grad_kernel = call(
        finish_kernel,
        (info, held, swap(held, "core", 1)),
        [((EROWS, FF), f32), ((RROWS, C), f32), ((KS, KS, C), f32)],
        name="finish",
    )
    return result[None], grad_tiles[None], grad_expand, grad_reduce, grad_kernel


def solution(mesh):
    fine = Mesh(mesh.devices.reshape(4, 4, 2, 8), ("y", "x", "core", "rep"))
    tiles = P("rep", TILE, None, None, None)
    placed = (
        tiles,
        tiles,
        P("rep", TILE, None),
        P("rep", TILE),
        P(),
        P(),
        P("rep", None),
        P(),
        P("rep", None),
    )
    return jax.shard_map(
        per_device,
        mesh=fine,
        in_specs=placed,
        out_specs=(tiles, tiles, P("rep", None), P("rep", None), P()),
        check_vma=False,
    )
```

```python
import functools

import jax
import jax.numpy as jnp
from jax import lax
from jax.experimental import pallas as pl
from jax.experimental.pallas import tpu as pltpu
from jax.sharding import Mesh, PartitionSpec as P

inv_root_two = 0.7071067811865476
inv_root_two_pi = 0.3989422804014327
bf16 = jnp.bfloat16
f32 = jnp.float32
REP_ORDER = (0, 7, 2, 5, 1, 6, 3, 4)
TILE = ("y", "x", "core")
SIZES = {"y": 4, "x": 4, "core": 2, "rep": 8}
C, FF, S, CAP, KS = 192, 768, 16, 4, 7
SIDE = 2 * S
TAPS = KS * KS
HALF = S + 6
WIDE = SIDE + 8
LANES = 128
TAIL = C - LANES
SHARD = C * FF // SIZES["rep"] // LANES
ROWS = SHARD * SIZES["rep"]
EROWS = C // SIZES["rep"]
RROWS = FF // SIZES["rep"]
GROWS = 48
FACTOR = 1.0 / 512.0
VMEM_LIMIT = 48 * 1024 * 1024


def swap(value, axis, bit):
    return lax.ppermute(value, axis, [(i, i ^ bit) for i in range(SIZES[axis])])


def bit_of(axis, bit):
    return (lax.axis_index(axis) // bit) % 2


def dot(left, right, contract):
    return lax.dot_general(left, right, ((contract[:1], contract[1:]), ((), ())), preferred_element_type=f32)


CORE, AT_REP, COUNT, PLACE = 0, 1, 2, 3


def place_kernel(info, tiles, canvas, sems):
    def tile_copy(j):
        p = info[0, PLACE + j]
        row = pl.multiple_of((p // 2) * S, S)
        col = pl.multiple_of((p % 2) * S, S)
        return row, col, pltpu.make_async_copy(
            tiles.at[j], canvas.at[pl.ds(row, S), pl.ds(col, S), :], sems.at[j]
        )

    for j in range(CAP):
        row, col, copy = tile_copy(j)

        @pl.when(j < info[0, COUNT])
        def _():
            copy.start()

        @pl.when(j >= info[0, COUNT])
        def _():
            canvas[pl.ds(row, S), pl.ds(col, S), :] = jnp.zeros((S, S, C), bf16)

    for j in range(CAP):

        @pl.when(j < info[0, COUNT])
        def _():
            tile_copy(j)[2].wait()


def pack_kernel(info, expand, project, packed):
    e, r = pack_expand(expand[...].astype(f32)), pack_reduce(project[...].astype(f32))
    packed[...] = jnp.where(info[0, CORE] == 0, e, r).astype(bf16)


def fill_taps(kernel, taps, flip):
    for dy in range(KS):
        for dx in range(KS):
            row = kernel[KS - 1 - dy, KS - 1 - dx : KS - dx] if flip else kernel[dy, dx : dx + 1]
            both = jnp.concatenate([row[:, LANES:], row[:, LANES:]], axis=1)
            taps[0, dy * KS + dx] = jnp.broadcast_to(row[:, :LANES], (8, LANES))
            taps[1, dy * KS + dx] = jnp.broadcast_to(both, (8, LANES))


def field_kernel(padded, kernel, planes, filtered, taps):
    fill_taps(kernel, taps, False)
    fill_planes(padded, planes)
    conv_planes(planes, taps, filtered)


def fill_planes(padded, planes):
    planes[0] = padded[:HALF, :, :LANES]
    planes[2] = padded[S:, :, :LANES]
    planes[1] = jnp.concatenate([padded[:HALF, :, LANES:], padded[S:, :, LANES:]], axis=-1)


def conv_planes(planes, taps, out, first=0, last=3):
    def body(step, carry):
        t = step // 4
        col = pl.multiple_of((step % 4) * 8, 8)
        acc = jnp.zeros((S, 8, LANES), f32)
        for dx in range(KS):
            x = planes[t, :, pl.ds(col + dx, 8), :]
            for dy in range(KS):
                acc = acc + x[dy : dy + S] * taps[t % 2, dy * KS + dx]
        out[t, :, pl.ds(col, 8), :] = acc
        return carry

    lax.fori_loop(4 * first, 4 * last, body, 0, unroll=4)


def correlate_planes(planes, field, acc):
    acc[...] = jnp.zeros_like(acc)

    def body(step, carry):
        t = step // 4
        col = pl.multiple_of((step % 4) * 8, 8)
        g = [field[t, row, pl.ds(col, 8), :] for row in range(S)]
        for dx in range(KS):
            sums = [None] * KS
            for row in range(HALF):
                x = planes[t, row, pl.ds(col + dx, 8), :]
                for dy in range(max(0, row - S + 1), min(KS, row + 1)):
                    term = x * g[row - dy]
                    sums[dy] = term if sums[dy] is None else sums[dy] + term
            for dy in range(KS):
                acc[t, dy * KS + dx] += sums[dy]
        return carry

    lax.fori_loop(0, 12, body, 0, unroll=2)


def tile_of(planes, p):
    lower = p // 2
    col = pl.multiple_of((p % 2) * S, S)
    main = planes[2 * lower, :, pl.ds(col, S), :].reshape(S * S, LANES)
    tail = planes[1, :, pl.ds(col, S), :].reshape(S * S, LANES)
    tail = jnp.where(lower == 1, pltpu.roll(tail, TAIL, 1), tail)
    return jnp.concatenate([main, tail[:, :TAIL]], axis=1)


def pack_expand(rows):
    return jnp.concatenate([rows[:, k * LANES : (k + 1) * LANES] for k in range(FF // LANES)], axis=0)


def pack_reduce(rows):
    half = RROWS // 2
    tails = jnp.concatenate([rows[:half, LANES:], rows[half:, LANES:]], axis=1)
    return jnp.concatenate([rows[:, :LANES], tails], axis=0)


def unpack_expand(value):
    return jnp.concatenate([value[k * EROWS : (k + 1) * EROWS] for k in range(FF // LANES)], axis=1)


def unpack_reduce(value):
    tail = value[RROWS:SHARD]
    tails = jnp.concatenate([tail[:, :TAIL], tail[:, TAIL:]], axis=0)
    return jnp.concatenate([value[:RROWS], tails], axis=1)


def split_high_low(value):
    high = value.astype(bf16)
    return high, (value - high.astype(f32)).astype(bf16)


def block_kernel(
    info, planes, filtered, tiles, cotan, gain, bias, held, other,
    result, field_out, keep, send, keep_taps,
    field, tap_acc, expand_wide, expand, project, hidden, active, grad_hidden,
    grad_e, grad_r, grad_rt,
):
    me, my_z = info[0, CORE], info[0, AT_REP]
    for k, s in enumerate(REP_ORDER):
        z = my_z ^ s
        mine, theirs = held[k].astype(f32), other[k].astype(f32)
        rows = pl.ds(pl.multiple_of(z * EROWS, 8), EROWS)
        expand_wide[rows, :] = unpack_expand(jnp.where(me == 0, mine, theirs))
        rows = pl.ds(pl.multiple_of(z * RROWS, RROWS), RROWS)
        project[rows, :] = unpack_reduce(jnp.where(me == 0, theirs, mine)).astype(bf16)
    expand[...] = expand_wide[...].astype(bf16)
    field[...] = jnp.zeros_like(field)
    field_out[...] = jnp.zeros_like(field_out)
    grad_e[...] = jnp.zeros_like(grad_e)
    grad_r[...] = jnp.zeros_like(grad_r)

    def slot(j):
        live = j < info[0, COUNT]
        p = info[0, PLACE + j]
        lower = p // 2
        row = pl.multiple_of(lower * S, S)
        col = pl.multiple_of((p % 2) * S, S)
        x = tile_of(filtered, p)
        spread = x - jnp.sum(x, axis=1, keepdims=True) * (1.0 / C)
        inverse = lax.rsqrt(jnp.sum(spread * spread, axis=1, keepdims=True) * (1.0 / C) + 1e-6)
        normed = spread * inverse
        scaled = (normed * gain[...]).astype(bf16)
        up = jnp.where(live, cotan[j].reshape(S * S, C), jnp.zeros((S * S, C), bf16))
        hidden[j, 0] = dot(scaled, expand[...], (1, 0))
        hidden[j, 1] = dot(up, project[...], (1, 1))

        def gelu(r, carry):
            rows = pl.ds(pl.multiple_of(r * 16, 16), 16)
            h = hidden[j, 0, rows, :] + bias[...]
            cdf = 0.5 * (1.0 + lax.erf(h * inv_root_two))
            slope = cdf + h * jnp.exp(-0.5 * h * h) * inv_root_two_pi
            active[j, rows, :] = (h * cdf).astype(bf16)
            grad_hidden[j, rows, :] = (hidden[j, 1, rows, :] * slope).astype(bf16)
            return carry

        lax.fori_loop(0, S, gelu, 0, unroll=S)
        a, gh = active[j], grad_hidden[j]
        mixed = dot(a, project[...], (1, 0))
        result[j] = jnp.where(live, tiles[j].astype(f32) + mixed.reshape(S, S, C), jnp.zeros((S, S, C), f32))
        grad_e[...] += dot(scaled, gh, (0, 0))
        grad_r[...] += dot(up, a, (0, 0))
        q = dot(gh, expand[...], (1, 1)) * gain[...]
        mean_q = jnp.sum(q, axis=1, keepdims=True) * (1.0 / C)
        mean_qn = jnp.sum(q * normed, axis=1, keepdims=True) * (1.0 / C)
        g = (inverse * (q - mean_q - normed * mean_qn)).astype(bf16)
        field_out[pl.ds(row, S), pl.ds(col, S), :] = g.reshape(S, S, C)
        g = g.astype(f32)
        field[2 * lower, :, pl.ds(col, S), :] = g[:, :LANES].reshape(S, S, LANES)
        tail = jnp.concatenate([g[:, LANES:], g[:, LANES:]], axis=1).reshape(S, S, LANES)
        old = field[1, :, pl.ds(col, S), :]
        side = lax.broadcasted_iota(jnp.int32, (S, S, LANES), 2) // TAIL
        field[1, :, pl.ds(col, S), :] = jnp.where(side == lower, tail, old)

    for j in range(CAP):
        slot(j)

    correlate_planes(planes, field, tap_acc)
    sums = jnp.sum(tap_acc[...], axis=2)
    main = sums[0] + sums[2]
    tail = sums[1] + pltpu.roll(sums[1], TAIL, 1)
    pad = jnp.zeros((7, LANES), f32)
    main = jnp.concatenate([main, pad], axis=0)
    tail = jnp.concatenate([tail, pad], axis=0)
    low_lane = lax.broadcasted_iota(jnp.int32, (16, LANES), 1) < TAIL
    halves = []
    for h in range(2):
        s = 24 * h
        tails = jnp.where(low_lane, tail[s : s + 16], tail[s + 16 : s + 32])
        halves.append(jnp.concatenate([main[s : s + 32], tails], axis=0))
    keep_taps[...] = jnp.where(me == 0, halves[0], halves[1])
    high, low = split_high_low(jnp.where(me == 0, halves[1], halves[0]))
    send[ROWS : ROWS + GROWS] = high
    send[ROWS + GROWS :] = low
    grad_rt[...] = grad_r[...].T
    for k, s in enumerate(REP_ORDER):
        z = my_z ^ s
        e = pack_expand(grad_e[pl.ds(pl.multiple_of(z * EROWS, 8), EROWS), :])
        r = pack_reduce(grad_rt[pl.ds(pl.multiple_of(z * RROWS, RROWS), RROWS), :])
        keep[k * SHARD : (k + 1) * SHARD] = jnp.where(me == 0, e, r)
        send[k * SHARD : (k + 1) * SHARD] = jnp.where(me == 0, r, e).astype(bf16)


def finish_kernel(info, held, other, grad_e, grad_r, grad_k):
    first = info[0, CORE] == 0
    grad_e[...] = unpack_expand(jnp.where(first, held[:SHARD], other[:SHARD])) * FACTOR
    grad_r[...] = unpack_reduce(jnp.where(first, other[:SHARD], held[:SHARD])) * FACTOR
    a, b = held[SHARD:], other[SHARD:]
    halves = []
    for half in (jnp.where(first, a, b), jnp.where(first, b, a)):
        tails = jnp.concatenate([half[32:, :TAIL], half[32:, TAIL:]], axis=0)
        halves.append(jnp.concatenate([half[:32], tails], axis=1))
    whole = jnp.concatenate([halves[0][:24], halves[1]], axis=0) * FACTOR
    for dy in range(KS):
        grad_k[dy] = whole[dy * KS : (dy + 1) * KS]


def spread_kernel(padded, kernel, planes, summed, taps):
    fill_taps(kernel, taps, True)
    fill_planes(padded, planes)
    conv_planes(planes, taps, summed, 0, 2)


def emit_kernel(info, planes, partial, cotan, kernel, out, summed, taps):
    fill_taps(kernel, taps, True)
    summed[:2] = partial[:2]
    conv_planes(planes, taps, summed, 2, 3)

    def blank(j, carry):
        out[j] = jnp.zeros_like(out[j])
        return carry

    lax.fori_loop(info[0, COUNT], CAP, blank, 0)

    def slot(j, carry):
        out[j] = cotan[j].astype(f32) + tile_of(summed, info[0, PLACE + j]).reshape(S, S, C)
        return carry

    lax.fori_loop(0, info[0, COUNT], slot, 0)


def call(kernel, ins, outs, scratch=(), name=None, us=1):
    smem = pl.BlockSpec(memory_space=pltpu.SMEM)
    vmem = pl.BlockSpec(memory_space=pltpu.VMEM)
    specs = [smem if v.dtype == jnp.int32 else vmem for v in ins]
    return pl.pallas_call(
        kernel,
        out_shape=[jax.ShapeDtypeStruct(shape, dtype) for shape, dtype in outs],
        in_specs=specs,
        out_specs=[vmem for _ in outs],
        scratch_shapes=[pltpu.VMEM(*s) if isinstance(s, tuple) else s for s in scratch],
        compiler_params=pltpu.CompilerParams(vmem_limit_bytes=VMEM_LIMIT),
        cost_estimate=pl.CostEstimate(flops=us * 10**9, bytes_accessed=us * 10**6, transcendentals=0),
        name=name,
    )(*ins)


TAP_PLANES = (2, TAPS, 8, LANES)
PLANES, CELLS = (3, HALF, WIDE, LANES), (3, S, SIDE, LANES)


def block_call(*ins):
    return call(
        block_kernel,
        ins,
        [
            ((CAP, S, S, C), f32),
            ((SIDE, SIDE, C), bf16),
            ((ROWS, LANES), f32),
            ((ROWS + 2 * GROWS, LANES), bf16),
            ((GROWS, LANES), f32),
        ],
        [
            (CELLS, f32),
            ((3, TAPS, 8, LANES), f32),
            ((C, FF), f32),
            ((C, FF), bf16),
            ((FF, C), bf16),
            ((CAP, 2, S * S, FF), f32),
            ((CAP, S * S, FF), bf16),
            ((CAP, S * S, FF), bf16),
            ((C, FF), f32),
            ((C, FF), f32),
            ((FF, C), f32),
        ],
        name="block",
        us=14,
    )


def side_rims(canvas):
    core = lax.axis_index("core")
    west_edge = canvas[:, :3].transpose(1, 0, 2)
    east_edge = canvas[:, -3:].transpose(1, 0, 2)
    inner = swap(jnp.where(core == 0, east_edge, west_edge), "core", 1)
    pairs = [(4 * i + a, 4 * i + 3 - a) for i in range(2) for a in range(4)]
    outer = lax.ppermute(jnp.where(core == 0, west_edge, east_edge), ("x", "core"), pairs)
    return inner, jnp.where(lax.axis_index("x") % 2 != core, outer, jnp.zeros_like(outer))


def widen(canvas, inner, outer):
    core = lax.axis_index("core")
    west = jnp.where(core == 0, outer, inner).transpose(1, 0, 2)
    east = jnp.where(core == 0, inner, outer).transpose(1, 0, 2)
    blank = jnp.zeros((SIDE, WIDE - SIDE - 6, C), canvas.dtype)
    return jnp.concatenate([west, canvas, east, blank], axis=1)


def end_rims(widened):
    upper = lax.axis_index("x") // 2
    north_edge, south_edge = widened[:3], widened[-3:]
    near = swap(jnp.where(upper == 0, south_edge, north_edge), "x", 2)
    pairs = [(4 * y + x, 4 * ((y + 1) % 4) + x - 2) for y in range(4) for x in (2, 3)]
    far = lax.ppermute(
        jnp.where(upper == 0, north_edge, south_edge),
        ("y", "x"),
        pairs + [(b, a) for a, b in pairs],
    )
    inside = jnp.where(upper == 0, lax.axis_index("y") > 0, lax.axis_index("y") < 3)
    return near, jnp.where(inside, far, jnp.zeros_like(far))


def pad_ends(widened, near, far):
    upper = lax.axis_index("x") // 2
    north = jnp.where(upper == 0, far, near)
    south = jnp.where(upper == 0, near, far)
    return jnp.concatenate([north, widened, south], axis=0).astype(f32)


def tie(value, *others):
    return lax.optimization_barrier((value, *others))


def rows_sum(own, a, b, c):
    return (own + a) + (b + c)


def join(value):
    return value[:GROWS].astype(f32) + value[GROWS:].astype(f32)


def per_device(
    tile_data,
    cotangent,
    tile_place,
    tile_count,
    kernel,
    norm_gain,
    expand_weight,
    hidden_bias,
    reduce_weight,
):
    scalars = [lax.axis_index(a) for a in ("core", "rep")] + [tile_count[0, 0]]
    info = jnp.concatenate([jnp.stack(scalars).astype(jnp.int32), tile_place[0, 0]])[None]
    tiles, cotan = tile_data[0], cotangent[0]
    (canvas,) = call(
        place_kernel,
        (info, tiles),
        [((SIDE, SIDE, C), bf16)],
        [pltpu.SemaphoreType.DMA((CAP,))],
        name="place",
    )
    inner, outer = side_rims(canvas)
    shards, inner = tie(expand_weight, inner)
    (packed,) = call(
        pack_kernel, (info, shards, reduce_weight), [((SHARD, LANES), bf16)], name="pack", us=0
    )
    held = jnp.stack([packed, swap(packed, "rep", 7)])
    widened = widen(canvas, inner, outer)
    near, far = end_rims(widened)
    held = jnp.concatenate([held, swap(held, "rep", 2)])
    held_got = swap(held, "rep", 1)
    planes, filtered = call(
        field_kernel,
        (pad_ends(widened, near, far), kernel),
        [(PLANES, f32), (CELLS, f32)],
        [(TAP_PLANES, f32)],
        name="field",
        us=0,
    )
    held_got, filtered = tie(held_got, filtered)
    held = jnp.concatenate([held, held_got])
    other = swap(held, "core", 1)
    result, field, keep, send, taps = block_call(
        info,
        planes,
        filtered,
        tiles,
        cotan,
        norm_gain.reshape(1, C),
        hidden_bias.reshape(1, FF),
        held,
        other,
    )
    got = swap(send, "core", 1)
    inner, outer = side_rims(field)
    held = keep + got[:ROWS].astype(f32)
    taps = taps + join(got[ROWS:])

    def halve(held, taps, bits, *after):
        half = held.shape[0] // 2
        high, low = split_high_low(taps)
        part = jnp.concatenate([held[half:].astype(bf16), high, low])
        part = tie(part, *after)[0]
        got = swap(part, "rep", bits)
        return (
            held[:half] + got[:half].astype(f32),
            (high.astype(f32) + low.astype(f32)) + join(got[half:]),
        )

    got, inner = tie(got, inner)
    widened = widen(field, inner, outer)
    near, far = end_rims(widened)
    held, taps = halve(held, taps, 1)
    near = tie(near, held)[0]
    planes, summed = call(
        spread_kernel,
        (pad_ends(widened, near, far), kernel),
        [(PLANES, f32), (CELLS, f32)],
        [(TAP_PLANES, f32)],
        name="spread",
        us=0,
    )
    held, taps = halve(held, taps, 2)
    held, taps = halve(held, taps, 7, summed)
    (grad_tiles,) = call(
        emit_kernel,
        (info, planes, summed, cotan, kernel),
        [((CAP, S, S, C), f32)],
        [(CELLS, f32), (TAP_PLANES, f32)],
        name="emit",
        us=0,
    )
    taps, grad_tiles = tie(taps, grad_tiles)
    for axis in ("x", "y"):
        part = jnp.concatenate([held.astype(bf16), *split_high_low(taps)])
        parts = [part] + [swap(part, axis, i) for i in (2, 1, 3)]
        held = rows_sum(*[p[:SHARD].astype(f32) for p in parts])
        taps = rows_sum(*[join(p[SHARD:]) for p in parts])
    held = jnp.concatenate([held, taps])
    grad_expand, grad_reduce, grad_kernel = call(
        finish_kernel,
        (info, held, swap(held, "core", 1)),
        [((EROWS, FF), f32), ((RROWS, C), f32), ((KS, KS, C), f32)],
        name="finish",
    )
    return result[None], grad_tiles[None], grad_expand, grad_reduce, grad_kernel


def solution(mesh):
    fine = Mesh(mesh.devices.reshape(4, 4, 2, 8), ("y", "x", "core", "rep"))
    tiles = P("rep", TILE, None, None, None)
    placed = (
        tiles,
        tiles,
        P("rep", TILE, None),
        P("rep", TILE),
        P(),
        P(),
        P("rep", None),
        P(),
        P("rep", None),
    )
    return jax.shard_map(
        per_device,
        mesh=fine,
        in_specs=placed,
        out_specs=(tiles, tiles, P("rep", None), P("rep", None), P()),
        check_vma=False,
    )
```
